32 devices in a mesh: res: 8 (over y, x, core), frame: 4 (over z).
Axes of the slice: x: 2, y: 2, z: 4, core: 2. Of those that a mesh axis runs over, the one named last changes fastest.
Arguments:
- activations: bfloat16 [8, 1024, 768], P('frame', 'res'), may hold values from -6 to 6
- contacts: int32 [8, 5], replicated, may hold values from 0 to 1, as said below
- frame_index: int32 [8], replicated, may hold values from 0 to 21, as said below
- spatial_qkv: bfloat16 [768, 2304], replicated, may hold values from -8 to 8
- spatial_out: bfloat16 [768, 768], replicated, may hold values from -0.21875 to 0.21875
- time_qkv: bfloat16 [768, 2304], replicated, may hold values from -8 to 8
- time_out: bfloat16 [768, 768], replicated, may hold values from -0.21875 to 0.21875
Outputs:
- layer_out: bfloat16 [8, 1024, 768], P('frame', 'res')
The draws below stay inside these ranges and needn't reach their ends.
Inputs may be any that keep to these rules, and one draw needn't show every extreme that they name: contacts[b, 2] = 1 for every block; contacts are symmetric, contacts[b, 2 + d] = contacts[b + d, 2 - d]; flags that name a block outside 0 to 7 are 0. Strictly increasing, frame_index[0] = 0, frame_index[7] = 21.
All inputs are finite; a program needn't handle non-finite values.
Results may differ from the reference program's by a relative error of at most 0.025.
Values may be sent and summed in bfloat16 or wider, within the bound.
A program may use at most 128 MiB of HBM per device.

```python
import math
import jax
import jax.numpy as jnp
from jax import lax

D = 768
HEADS = 12
HEAD = 64
BLK = 128
HALO = 2
FRAMES = 8
NBLK = 8
RES = 1024


def projection_triple(base_key, coupling):
    query_key, keys_key, values_key, strength_key = jax.random.split(base_key, 4)
    spread = D ** (-0.5)
    query = jax.random.normal(query_key, (D, D), jnp.float32) * (2.0 * spread)
    values = jax.random.normal(values_key, (D, D), jnp.float32) * spread
    strength = jnp.exp(jax.random.uniform(strength_key, (HEADS,), jnp.float32) * math.log(16.0)) * coupling
    strength = jnp.repeat(strength, HEAD)
    keys = query * strength[None, :] + jax.random.normal(keys_key, (D, D), jnp.float32) * (2.0 * spread)
    return jnp.concatenate([query, keys, values], axis=1).astype(jnp.bfloat16)


def draw_spatial_qkv(key, part):
    key = jax.random.fold_in(key, 11)
    return projection_triple(key, 0.0)


def draw_time_qkv(key, part):
    key = jax.random.fold_in(key, 12)
    return projection_triple(key, 0.0)


def draw_contacts(key, part):
    key = jax.random.fold_in(key, 13)
    activity_key, pair_key = jax.random.split(key, 2)
    activity = jax.random.randint(activity_key, (NBLK,), 0, 4)
    pair_draws = jax.random.randint(pair_key, (NBLK, HALO), 0, 8)
    partner = jnp.arange(NBLK)[:, None] + jnp.arange(1, HALO + 1)[None, :]
    inside = partner < NBLK
    partner_activity = activity[jnp.minimum(partner, NBLK - 1)]
    linked = jnp.where((pair_draws < activity[:, None] + partner_activity + 1) & inside, 1, 0).astype(jnp.int32)
    columns = []
    for distance in range(HALO, 0, -1):
        columns.append(jnp.concatenate([jnp.zeros((distance,), jnp.int32), linked[:NBLK - distance, distance - 1]]))
    columns.append(jnp.ones((NBLK,), jnp.int32))
    for distance in range(1, HALO + 1):
        columns.append(linked[:, distance - 1])
    return jnp.stack(columns, axis=1)


def draw_frame_index(key, part):
    key = jax.random.fold_in(key, 14)
    strides = jax.random.randint(key, (FRAMES - 1,), 1, 4)
    leading = jnp.concatenate([jnp.zeros((1,), jnp.int32), jnp.cumsum(strides[:-1]).astype(jnp.int32)])
    closing = jnp.full((1,), 3 * FRAMES - 3, jnp.int32)
    return jnp.concatenate([leading, closing]).astype(jnp.int32)


def block_scale(rng, shape, cuts, low, high):
    loudness = 1.0
    for axis_at, blocks in cuts:
        steps = jax.random.uniform(jax.random.fold_in(jax.random.fold_in(rng, 6), axis_at), (blocks,), jnp.float32, low / len(cuts), high / len(cuts))
        loudness = loudness * jnp.repeat(jnp.exp(steps), shape[axis_at] // blocks).reshape((-1,) + (1,) * (len(shape) - 1 - axis_at))
    return loudness


def centred(key, shape, width, reach, shards=(), kind=jnp.bfloat16):
    values = jax.random.normal(key, shape, jnp.float32) * width
    if len(shards) > 0:
        values = block_scale(key, shape, shards, -0.22, 0.18) * values
    return jnp.clip(values, min=-reach, max=reach).astype(kind)


def setup_inputs(seed: int = 0) -> dict:
    seeds = jax.random.split(jax.random.key(seed), 8)
    return {
        "activations": centred(seeds[0], (FRAMES, RES, D), 1.0, 6.0, ((0, 4), (1, 8))),
        "contacts": draw_contacts(jax.random.fold_in(seeds[7], 71), 0),
        "frame_index": draw_frame_index(jax.random.fold_in(seeds[7], 71), 0),
        "spatial_qkv": draw_spatial_qkv(jax.random.fold_in(seeds[7], 71), 0),
        "spatial_out": centred(seeds[4], (D, D), D ** -0.5, 0.21875),
        "time_qkv": draw_time_qkv(jax.random.fold_in(seeds[7], 71), 0),
        "time_out": centred(seeds[6], (D, D), D ** -0.5, 0.21875),
    }


def normalize(values_in):
    widened = values_in.astype(jnp.float32)
    mean_square = lax.optimization_barrier(jnp.mean(widened * widened, axis=-1, keepdims=True))
    return (widened * lax.rsqrt(mean_square + 1e-06)).astype(jnp.bfloat16)

def rotate(entries, positions):
    half_size = HEAD // 2
    frequency = 10000.0 ** (-jnp.arange(half_size, dtype=jnp.float32) / half_size)
    angles = positions.astype(jnp.float32)[:, None] * frequency[None, :]
    cosine = jnp.cos(angles)[:, None, None, :]
    sine = jnp.sin(angles)[:, None, None, :]
    first = entries[..., :half_size]
    second = entries[..., half_size:]
    return jnp.concatenate([first * cosine - second * sine, first * sine + second * cosine], axis=-1)

def softmax_rounded(scores):
    top = lax.optimization_barrier(jnp.max(scores, axis=-1, keepdims=True))
    expo = jnp.exp(scores - top)
    weights = (expo / lax.optimization_barrier(jnp.sum(expo, axis=-1, keepdims=True))).astype(jnp.bfloat16)
    return lax.optimization_barrier(weights).astype(jnp.float32)

def time_attend(query, keys, values):
    score_scale = HEAD ** (-0.5)
    scores = jnp.einsum('frhd,grhd->rhfg', query.astype(jnp.float32), keys.astype(jnp.float32)) * score_scale
    weights = softmax_rounded(scores)
    return jnp.einsum('rhfg,grhd->frhd', weights, values.astype(jnp.float32)).astype(jnp.bfloat16)

def reference(activations, contacts, frame_index, spatial_qkv, spatial_out, time_qkv, time_out):
    frame_count, residues, model_width = activations.shape
    head_count = model_width // HEAD
    block_count = residues // BLK
    score_scale = HEAD ** (-0.5)
    flat = activations.reshape(frame_count * residues, model_width)
    normed = normalize(flat)
    projected = jnp.dot(normed, spatial_qkv, preferred_element_type=jnp.float32).astype(jnp.bfloat16)
    projected = projected.reshape(frame_count, block_count, BLK, 3, head_count, HEAD)

    def spatial_frame(frame_proj):
        query = frame_proj[:, :, 0].astype(jnp.float32)
        keys = frame_proj[:, :, 1].astype(jnp.float32)
        values = frame_proj[:, :, 2].astype(jnp.float32)
        padding = ((HALO, HALO), (0, 0), (0, 0), (0, 0))
        keys_padded = jnp.pad(keys, padding)
        values_padded = jnp.pad(values, padding)
        score_list = []
        for column in range(2 * HALO + 1):
            tile = jnp.einsum('brhd,bshd->bhrs', query, keys_padded[column:column + block_count]) * score_scale
            allowed = contacts[:, column][:, None, None, None] > 0
            score_list.append(jnp.where(allowed, tile, -1e+30))
        weights = softmax_rounded(jnp.concatenate(score_list, axis=-1))
        result = jnp.zeros((block_count, BLK, head_count, HEAD), jnp.float32)
        for column in range(2 * HALO + 1):
            part_weights = weights[..., column * BLK:(column + 1) * BLK]
            result = result + jnp.einsum('bhrs,bshd->brhd', part_weights, values_padded[column:column + block_count])
        return result.astype(jnp.bfloat16)
    spatial_mix = lax.map(spatial_frame, projected).reshape(frame_count * residues, model_width)
    hidden = (flat.astype(jnp.float32) + jnp.dot(spatial_mix, spatial_out, preferred_element_type=jnp.float32)).astype(jnp.bfloat16)
    renormed = normalize(hidden)
    time_projected = jnp.dot(renormed, time_qkv, preferred_element_type=jnp.float32).astype(jnp.bfloat16)
    time_projected = time_projected.reshape(frame_count, residues, 3, head_count, HEAD)
    query = rotate(time_projected[:, :, 0].astype(jnp.float32), frame_index).astype(jnp.bfloat16)
    keys = rotate(time_projected[:, :, 1].astype(jnp.float32), frame_index).astype(jnp.bfloat16)
    values = time_projected[:, :, 2]

    def to_blocks(entries):
        return jnp.transpose(entries.reshape(frame_count, block_count, BLK, head_count, HEAD), (1, 0, 2, 3, 4))

    def time_block(operands):
        return time_attend(operands[0], operands[1], operands[2])
    time_mix = lax.map(time_block, (to_blocks(query), to_blocks(keys), to_blocks(values)))
    time_mix = jnp.transpose(time_mix, (1, 0, 2, 3, 4)).reshape(frame_count * residues, model_width)
    layer_out = hidden.astype(jnp.float32) + jnp.dot(time_mix, time_out, preferred_element_type=jnp.float32)
    return layer_out.astype(jnp.bfloat16).reshape(frame_count, residues, model_width)
```

```python
import functools
import math

import jax
import jax.numpy as jnp
from jax import lax
from jax.experimental import pallas as pl
from jax.experimental.pallas import tpu as pltpu
from jax.sharding import PartitionSpec as P

HEAD = 64
HALO = 2
PAIR = 2 * HEAD
OWN, NEAR, BELOW, ABOVE, FAR = range(5)
F32 = jnp.float32
BF16 = jnp.bfloat16


def normalize(values_in):
    widened = values_in.astype(F32)
    mean_square = jnp.mean(widened * widened, axis=-1, keepdims=True)
    return (widened * lax.rsqrt(mean_square + 1e-06)).astype(BF16)


def attend(query, keys, values, bias):
    rows = query.shape[0]
    lanes = lax.broadcasted_iota(jnp.int32, (1, PAIR), 1)
    first = jnp.where(lanes < HEAD, HEAD ** (-0.5), 0.0).astype(BF16)
    second = jnp.where(lanes < HEAD, 0.0, HEAD ** (-0.5)).astype(BF16)
    both = jnp.concatenate([query * first, query * second], axis=0)
    scores = (
        lax.dot_general(both, keys, (((1,), (1,)), ((), ())), preferred_element_type=F32) + bias
    )
    top = jnp.max(scores, axis=-1, keepdims=True)
    expo = jnp.exp(scores - top).astype(BF16)
    wide = jnp.concatenate([values, jnp.ones_like(values)], axis=1)
    mixed = jnp.dot(expo, wide, preferred_element_type=F32)
    low = lax.broadcasted_iota(jnp.int32, (rows, PAIR), 1) < HEAD
    total = jnp.where(low, mixed[:rows, :PAIR], mixed[rows:, :PAIR])
    count = jnp.where(low, mixed[:rows, PAIR:], mixed[rows:, PAIR:])
    return (total / count).astype(BF16)


def kernel(
    res_size, frame_size,
    acts, contacts, frame_index, sqkv_in, sout_in, tqkv_in, tout_in, out_ref,
    sqkv, sout, tqkv, tout, near, query, keys, values, mix, hidden, gathered, staged, landed,
    tquery, tkeys, tvalues, cosine, sine, same,
    weight_sem, halo_send, halo_recv, frame_send, frame_recv, back_send, back_recv,
):
    frames_dev, block, width = acts.shape
    heads = width // PAIR
    share = block // frame_size
    frames = frames_dev * frame_size
    chunk = frames_dev * share
    me = lax.axis_index("res")
    slot = lax.axis_index("frame")
    odd = lax.rem(me, 2)
    mate = me + 1 - 2 * odd
    has_below = me >= HALO
    has_above = me < res_size - HALO
    has_far = jnp.where(odd == 1, me + 1 < res_size, me >= 1)
    gives_far = jnp.where(odd == 1, has_below, has_above)

    weights = [
        pltpu.make_async_copy(source, target, weight_sem.at[i])
        for i, (source, target) in enumerate(
            [(sqkv_in, sqkv), (sout_in, sout), (tqkv_in, tqkv), (tout_in, tout)]
        )
    ]
    for copy in weights:
        copy.start()

    barrier = pltpu.get_barrier_semaphore()

    def greet(res, frame):
        pl.semaphore_signal(
            barrier, inc=1, device_id=(res, frame), device_id_type=pl.DeviceIdType.MESH
        )

    greet(mate, slot)

    @pl.when(has_below)
    def _():
        greet(me - HALO, slot)

    @pl.when(has_above)
    def _():
        greet(me + HALO, slot)

    for step in range(1, frame_size):
        greet(me, lax.rem(slot + step, frame_size))

    for f in range(frames_dev):
        near[f, OWN] = normalize(acts[f])

    pl.semaphore_wait(
        barrier, frame_size + has_below.astype(jnp.int32) + has_above.astype(jnp.int32)
    )

    def halo(f, source, target, place):
        return pltpu.make_async_remote_copy(
            src_ref=near.at[f, source],
            dst_ref=near.at[f, place],
            send_sem=halo_send.at[f, place],
            recv_sem=halo_recv.at[f, place],
            device_id=(target, slot),
            device_id_type=pl.DeviceIdType.MESH,
        )

    def to_mate(f):
        return halo(f, OWN, mate, NEAR)

    def to_above(f):
        return halo(f, OWN, me + HALO, BELOW)

    def to_below(f):
        return halo(f, OWN, me - HALO, ABOVE)

    def hand_on(f):
        return halo(f, ABOVE - odd, mate, FAR)

    for f in range(frames_dev):

        @pl.when(has_above)
        def _():
            to_above(f).start()

        @pl.when(has_below)
        def _():
            to_below(f).start()

        to_mate(f).start()

    for place, there in ((BELOW, has_below), (ABOVE, has_above), (FAR, has_far)):

        @pl.when(jnp.logical_not(there))
        def _():
            near[:, place] = jnp.zeros((frames_dev, block, width), BF16)

    size = frames * share
    lane = lax.broadcasted_iota(jnp.int32, (frames, PAIR), 1)
    row = lax.broadcasted_iota(jnp.int32, (frames, PAIR), 0)
    frequency = jnp.exp(lax.rem(lane, HEAD // 2).astype(F32) * (-math.log(10000.0) / (HEAD // 2)))
    position = jnp.zeros((frames, PAIR), F32)
    for g in range(frames):
        position = jnp.where(row == g, frame_index[g].astype(F32), position)
    angle = position * frequency
    for table, entries in ((cosine, jnp.cos(angle)), (sine, jnp.sin(angle))):
        table[...] = jnp.broadcast_to(entries[:, None, :], (frames, share, PAIR)).reshape(
            size, PAIR
        )
    row = lax.broadcasted_iota(jnp.int32, (2 * chunk, size), 0)
    column = lax.broadcasted_iota(jnp.int32, (2 * chunk, size), 1)
    same[...] = jnp.where(lax.rem(row, share) == lax.rem(column, share), 0.0, -1e30)
    row = lax.broadcasted_iota(jnp.int32, (PAIR, PAIR), 0)
    column = lax.broadcasted_iota(jnp.int32, (PAIR, PAIR), 1)
    upper = lax.rem(column, HEAD) >= HEAD // 2
    turn = jnp.where(
        upper,
        jnp.where(row == column - HEAD // 2, 1.0, 0.0),
        jnp.where(row == column + HEAD // 2, -1.0, 0.0),
    ).astype(BF16)
    order = (HALO, 3 - 2 * odd, 0, 2 * HALO, 1 + 2 * odd)
    bias = jnp.concatenate(
        [
            jnp.full((1, block), jnp.where(contacts[me, place] > 0, 0.0, -1e30), F32)
            for place in order
        ],
        axis=1,
    )

    def project(f, first, count):
        rows = near[f, first : first + count].reshape(count * block, width)
        span = slice(first * block, (first + count) * block)
        for part, target in ((1, keys), (2, values)):
            target[f, span] = jnp.dot(
                rows, sqkv[:, part * width : (part + 1) * width], preferred_element_type=F32
            ).astype(BF16)

    weights[0].wait()
    for f in range(frames_dev):
        query[f] = jnp.dot(near[f, OWN], sqkv[:, :width], preferred_element_type=F32).astype(BF16)
        to_mate(f).wait_recv()
        project(f, OWN, 2)

    def frame_copy(f, step):
        peer = lax.rem(slot + step, frame_size)
        return pltpu.make_async_remote_copy(
            src_ref=hidden.at[f, pl.ds(pl.multiple_of(peer * share, 16), share)],
            dst_ref=gathered.at[slot * frames_dev + f],
            send_sem=frame_send.at[f, peer],
            recv_sem=frame_recv.at[f, slot],
            device_id=(me, peer),
            device_id_type=pl.DeviceIdType.MESH,
        )

    def frame_arrival(f, step):
        peer = lax.rem(slot + step, frame_size)
        return pltpu.make_async_remote_copy(
            src_ref=hidden.at[f, pl.ds(0, share)],
            dst_ref=gathered.at[peer * frames_dev + f],
            send_sem=frame_send.at[f, peer],
            recv_sem=frame_recv.at[f, peer],
            device_id=(me, peer),
            device_id_type=pl.DeviceIdType.MESH,
        )

    mine = pl.ds(pl.multiple_of(slot * share, 16), share)
    for f in range(frames_dev):

        @pl.when(has_below)
        def _():
            to_above(f).wait_recv()

        @pl.when(has_above)
        def _():
            to_below(f).wait_recv()

        @pl.when(gives_far)
        def _():
            hand_on(f).start()

        project(f, BELOW, 2)

        @pl.when(has_far)
        def _():
            hand_on(f).wait_recv()

        project(f, FAR, 1)
        for pair in range(heads):
            span = slice(pair * PAIR, (pair + 1) * PAIR)
            mix[:, span] = attend(query[f, :, span], keys[f, :, span], values[f, :, span], bias)
        if f == 0:
            weights[1].wait()
        hidden[f] = (
            acts[f].astype(F32) + jnp.dot(mix[...], sout[...], preferred_element_type=F32)
        ).astype(BF16)
        for step in range(1, frame_size):
            frame_copy(f, step).start()
        gathered[slot * frames_dev + f] = hidden[f, mine]

    weights[2].wait()
    weights[3].wait()
    for f in range(frames_dev):
        for step in range(1, frame_size):
            frame_arrival(f, step).wait_recv()
    renormed = normalize(gathered[...].reshape(size, width))
    for part, target in ((0, tquery), (1, tkeys), (2, tvalues)):
        projected = jnp.dot(
            renormed, tqkv[:, part * width : (part + 1) * width], preferred_element_type=F32
        ).astype(BF16)
        if part == 2:
            target[...] = projected
        else:
            for pair in range(heads):
                span = slice(pair * PAIR, (pair + 1) * PAIR)
                piece = projected[:, span]
                turned = jnp.dot(piece, turn, preferred_element_type=F32)
                target[:, span] = (
                    piece.astype(F32) * cosine[...] + turned * sine[...]
                ).astype(BF16)

    def back_copy(step):
        peer = lax.rem(slot + step, frame_size)
        return pltpu.make_async_remote_copy(
            src_ref=staged.at[peer],
            dst_ref=landed.at[:, mine],
            send_sem=back_send.at[peer],
            recv_sem=back_recv.at[slot],
            device_id=(me, peer),
            device_id_type=pl.DeviceIdType.MESH,
        )

    def back_arrival(step):
        peer = lax.rem(slot + step, frame_size)
        return pltpu.make_async_remote_copy(
            src_ref=staged.at[peer],
            dst_ref=landed.at[:, pl.ds(pl.multiple_of(peer * share, 16), share)],
            send_sem=back_send.at[peer],
            recv_sem=back_recv.at[peer],
            device_id=(me, peer),
            device_id_type=pl.DeviceIdType.MESH,
        )

    def finish(step, carry):
        peer = lax.rem(slot + step, frame_size)
        rows = pl.ds(pl.multiple_of(peer * chunk, 16), chunk)
        parts = []
        for pair in range(heads):
            span = slice(pair * PAIR, (pair + 1) * PAIR)
            parts.append(attend(tquery[rows, span], tkeys[:, span], tvalues[:, span], same[...]))
        time_mix = jnp.concatenate(parts, axis=1)
        before = gathered[pl.ds(peer * frames_dev, frames_dev)].reshape(chunk, width)
        after = (
            before.astype(F32) + jnp.dot(time_mix, tout[...], preferred_element_type=F32)
        ).astype(BF16)
        staged[peer] = after.reshape(frames_dev, share, width)

        @pl.when(step < frame_size)
        def _():
            back_copy(step).start()

        return carry

    lax.fori_loop(1, frame_size + 1, finish, 0)
    landed[:, mine] = staged[slot]
    for step in range(1, frame_size):
        back_arrival(step).wait_recv()
    out_ref[...] = landed[...]

    for f in range(frames_dev):
        to_mate(f).wait_send()

        @pl.when(has_above)
        def _():
            to_above(f).wait_send()

        @pl.when(has_below)
        def _():
            to_below(f).wait_send()

        @pl.when(gives_far)
        def _():
            hand_on(f).wait_send()

        for step in range(1, frame_size):
            frame_copy(f, step).wait_send()
    for step in range(1, frame_size):
        back_copy(step).wait_send()


def solution(mesh):
    res_size, frame_size = mesh.shape["res"], mesh.shape["frame"]

    def shards(activations, contacts, frame_index, spatial_qkv, spatial_out, time_qkv, time_out):
        frames_dev, block, width = activations.shape
        share = block // frame_size
        frames = frames_dev * frame_size
        size = frames * share
        vmem = pl.BlockSpec(memory_space=pltpu.VMEM)
        smem = pl.BlockSpec(memory_space=pltpu.SMEM)
        hbm = pl.BlockSpec(memory_space=pl.ANY)
        dma = pltpu.SemaphoreType.DMA
        return pl.pallas_call(
            functools.partial(kernel, res_size, frame_size),
            out_shape=jax.ShapeDtypeStruct((frames_dev, block, width), BF16),
            in_specs=[vmem, smem, smem, hbm, hbm, hbm, hbm],
            out_specs=vmem,
            scratch_shapes=[
                pltpu.VMEM(spatial_qkv.shape, BF16),
                pltpu.VMEM(spatial_out.shape, BF16),
                pltpu.VMEM(time_qkv.shape, BF16),
                pltpu.VMEM(time_out.shape, BF16),
                pltpu.VMEM((frames_dev, 5, block, width), BF16),
                pltpu.VMEM((frames_dev, block, width), BF16),
                pltpu.VMEM((frames_dev, 5 * block, width), BF16),
                pltpu.VMEM((frames_dev, 5 * block, width), BF16),
                pltpu.VMEM((block, width), BF16),
                pltpu.VMEM((frames_dev, block, width), BF16),
                pltpu.VMEM((frames, share, width), BF16),
                pltpu.VMEM((frame_size, frames_dev, share, width), BF16),
                pltpu.VMEM((frames_dev, block, width), BF16),
                pltpu.VMEM((size, width), BF16),
                pltpu.VMEM((size, width), BF16),
                pltpu.VMEM((size, width), BF16),
                pltpu.VMEM((size, PAIR), F32),
                pltpu.VMEM((size, PAIR), F32),
                pltpu.VMEM((2 * frames_dev * share, size), F32),
                dma((4,)),
                dma((frames_dev, 5)),
                dma((frames_dev, 5)),
                dma((frames_dev, frame_size)),
                dma((frames_dev, frame_size)),
                dma((frame_size,)),
                dma((frame_size,)),
            ],
            compiler_params=pltpu.CompilerParams(
                collective_id=0, has_side_effects=True, vmem_limit_bytes=48 * 1024 * 1024
            ),
        )(activations, contacts, frame_index, spatial_qkv, spatial_out, time_qkv, time_out)

    placed = (P("frame", "res", None), P(), P(), P(), P(), P(), P())
    return jax.shard_map(
        shards, mesh=mesh, in_specs=placed, out_specs=P("frame", "res", None), check_vma=False
    )
```

```python
import functools
import math

import jax
import jax.numpy as jnp
from jax import lax
from jax.experimental import pallas as pl
from jax.experimental.pallas import tpu as pltpu
from jax.sharding import PartitionSpec as P

HEAD = 64
HALO = 2
PAIR = 2 * HEAD
OWN, NEAR, DIRECT, RELAYED, FAR = range(5)
F32 = jnp.float32
BF16 = jnp.bfloat16


def exclusive(first, second, size):
    bits = [1 << i for i in range(size.bit_length() - 1)]
    return sum(((first // w + second // w) % 2) * w for w in bits)


def normalize(values_in):
    widened = values_in.astype(F32)
    mean_square = jnp.mean(widened * widened, axis=-1, keepdims=True)
    return (widened * lax.rsqrt(mean_square + 1e-06)).astype(BF16)


def attend(query, keys, values, bias):
    rows = query.shape[0]
    lanes = lax.broadcasted_iota(jnp.int32, (1, PAIR), 1)
    first = jnp.where(lanes < HEAD, HEAD ** (-0.5), 0.0).astype(BF16)
    second = jnp.where(lanes < HEAD, 0.0, HEAD ** (-0.5)).astype(BF16)
    both = jnp.concatenate([query * first, query * second], axis=0)
    scores = (
        lax.dot_general(both, keys, (((1,), (1,)), ((), ())), preferred_element_type=F32) + bias
    )
    top = jnp.max(scores, axis=-1, keepdims=True)
    expo = jnp.exp(scores - top).astype(BF16)
    wide = jnp.concatenate([values, jnp.ones_like(values)], axis=1)
    mixed = jnp.dot(expo, wide, preferred_element_type=F32)
    low = lax.broadcasted_iota(jnp.int32, (rows, PAIR), 1) < HEAD
    total = jnp.where(low, mixed[:rows, :PAIR], mixed[rows:, :PAIR])
    count = jnp.where(low, mixed[:rows, PAIR:], mixed[rows:, PAIR:])
    return (total / count).astype(BF16)


def kernel(
    res_size, frame_size,
    acts_in, contacts, frame_index, sqkv_in, sout_in, tqkv_in, tout_in, out_ref,
    acts, sqkv, sout, tqkv, tout, near, query, keys, values, mix, hidden, gathered, staged, landed,
    tquery, tkeys, tvalues, cosine, sine, same,
    weight_sem, halo_send, halo_recv, frame_send, frame_recv, back_send, back_recv,
):
    frames_dev, block, width = acts.shape
    heads = width // PAIR
    share = block // frame_size
    frames = frames_dev * frame_size
    chunk = frames_dev * share
    me = lax.axis_index("res")
    slot = lax.axis_index("frame")
    odd = lax.rem(me, 2)
    side = lax.rem(me // 2, 2)
    mate = me + 1 - 2 * odd
    across = me + 2 - 4 * side
    relay_target = me + 4 - 8 * side
    relay_source = me - 4 + 8 * side
    gives_relay = jnp.logical_and(relay_target >= 0, relay_target < res_size)
    has_relayed = jnp.logical_and(relay_source >= 0, relay_source < res_size)
    gives_direct = side == odd
    gives_relayed = jnp.logical_and(side != odd, has_relayed)
    has_far = jnp.logical_or(side != odd, has_relayed)

    weights = [
        pltpu.make_async_copy(source, target, weight_sem.at[i])
        for i, (source, target) in enumerate(
            [(sqkv_in, sqkv), (sout_in, sout), (tqkv_in, tqkv), (tout_in, tout)]
        )
    ]
    fetch = pltpu.make_async_copy(acts_in, acts, weight_sem.at[4])
    fetch.start()
    for copy in weights:
        copy.start()

    barrier = pltpu.get_barrier_semaphore()

    def greet(res, frame):
        pl.semaphore_signal(
            barrier, inc=1, device_id=(res, frame), device_id_type=pl.DeviceIdType.MESH
        )

    greet(mate, slot)
    greet(across, slot)

    @pl.when(gives_relay)
    def _():
        greet(relay_target, slot)

    @pl.when(has_relayed)
    def _():
        greet(relay_source, slot)

    for step in range(1, frame_size):
        greet(me, exclusive(slot, step, frame_size))

    fetch.wait()
    for f in range(frames_dev):
        near[f, OWN] = normalize(acts[f])

    pl.semaphore_wait(
        barrier, frame_size + 1 + gives_relay.astype(jnp.int32) + has_relayed.astype(jnp.int32)
    )

    def halo(f, source, target, place):
        return pltpu.make_async_remote_copy(
            src_ref=near.at[f, source],
            dst_ref=near.at[f, place],
            send_sem=halo_send.at[f, place],
            recv_sem=halo_recv.at[f, place],
            device_id=(target, slot),
            device_id_type=pl.DeviceIdType.MESH,
        )

    def to_mate(f):
        return halo(f, OWN, mate, NEAR)

    def to_across(f):
        return halo(f, OWN, across, DIRECT)

    def relay(f):
        return halo(f, DIRECT, relay_target, RELAYED)

    def hand_on(f):
        return halo(f, DIRECT + side + odd - 2 * side * odd, mate, FAR)

    for f in range(frames_dev):
        to_across(f).start()
        to_mate(f).start()

    for place, there in ((RELAYED, has_relayed), (FAR, has_far)):

        @pl.when(jnp.logical_not(there))
        def _():
            near[:, place] = jnp.zeros((frames_dev, block, width), BF16)

    size = frames * share
    lane = lax.broadcasted_iota(jnp.int32, (frames, PAIR), 1)
    row = lax.broadcasted_iota(jnp.int32, (frames, PAIR), 0)
    frequency = jnp.exp(lax.rem(lane, HEAD // 2).astype(F32) * (-math.log(10000.0) / (HEAD // 2)))
    position = jnp.zeros((frames, PAIR), F32)
    for g in range(frames):
        position = jnp.where(row == g, frame_index[g].astype(F32), position)
    angle = position * frequency
    for table, entries in ((cosine, jnp.cos(angle)), (sine, jnp.sin(angle))):
        table[...] = jnp.broadcast_to(entries[:, None, :], (frames, share, PAIR)).reshape(
            size, PAIR
        )
    row = lax.broadcasted_iota(jnp.int32, (2 * chunk, size), 0)
    column = lax.broadcasted_iota(jnp.int32, (2 * chunk, size), 1)
    same[...] = jnp.where(lax.rem(row, share) == lax.rem(column, share), 0.0, -1e30)
    row = lax.broadcasted_iota(jnp.int32, (PAIR, PAIR), 0)
    column = lax.broadcasted_iota(jnp.int32, (PAIR, PAIR), 1)
    upper = lax.rem(column, HEAD) >= HEAD // 2
    turn = jnp.where(
        upper,
        jnp.where(row == column - HEAD // 2, 1.0, 0.0),
        jnp.where(row == column + HEAD // 2, -1.0, 0.0),
    ).astype(BF16)
    order = (HALO, 3 - 2 * odd, 2 * HALO * (1 - side), 2 * HALO * side, 1 + 2 * odd)
    bias = jnp.concatenate(
        [
            jnp.full((1, block), jnp.where(contacts[me, place] > 0, 0.0, -1e30), F32)
            for place in order
        ],
        axis=1,
    )

    def project(f, first, count):
        rows = near[f, first : first + count].reshape(count * block, width)
        span = slice(first * block, (first + count) * block)
        for part, target in ((1, keys), (2, values)):
            target[f, span] = jnp.dot(
                rows, sqkv[:, part * width : (part + 1) * width], preferred_element_type=F32
            ).astype(BF16)

    def pass_on(f):
        to_across(f).wait_recv()

        @pl.when(gives_relay)
        def _():
            relay(f).start()

        @pl.when(gives_direct)
        def _():
            hand_on(f).start()

    weights[0].wait()
    for f in range(frames_dev):
        query[f] = jnp.dot(near[f, OWN], sqkv[:, :width], preferred_element_type=F32).astype(BF16)
        to_mate(f).wait_recv()
        project(f, OWN, 2)
        if f == 0:
            pass_on(0)
    project(0, DIRECT, 1)
    for f in range(1, frames_dev):
        pass_on(f)
        project(f, DIRECT, 1)

    def frame_copy(f, step):
        peer = exclusive(slot, step, frame_size)
        return pltpu.make_async_remote_copy(
            src_ref=hidden.at[f, pl.ds(pl.multiple_of(peer * share, 16), share)],
            dst_ref=gathered.at[slot * frames_dev + f],
            send_sem=frame_send.at[f, peer],
            recv_sem=frame_recv.at[f, slot],
            device_id=(me, peer),
            device_id_type=pl.DeviceIdType.MESH,
        )

    def frame_arrival(f, step):
        peer = exclusive(slot, step, frame_size)
        return pltpu.make_async_remote_copy(
            src_ref=hidden.at[f, pl.ds(0, share)],
            dst_ref=gathered.at[peer * frames_dev + f],
            send_sem=frame_send.at[f, peer],
            recv_sem=frame_recv.at[f, peer],
            device_id=(me, peer),
            device_id_type=pl.DeviceIdType.MESH,
        )

    mine = pl.ds(pl.multiple_of(slot * share, 16), share)
    for f in range(frames_dev):

        @pl.when(has_relayed)
        def _():
            relay(f).wait_recv()

        @pl.when(gives_relayed)
        def _():
            hand_on(f).start()

        project(f, RELAYED, 1)

        @pl.when(has_far)
        def _():
            hand_on(f).wait_recv()

        project(f, FAR, 1)
        for pair in range(heads):
            span = slice(pair * PAIR, (pair + 1) * PAIR)
            mix[:, span] = attend(query[f, :, span], keys[f, :, span], values[f, :, span], bias)
        if f == 0:
            weights[1].wait()
        hidden[f] = (
            acts[f].astype(F32) + jnp.dot(mix[...], sout[...], preferred_element_type=F32)
        ).astype(BF16)
        for step in range(1, frame_size):
            frame_copy(f, step).start()
        gathered[slot * frames_dev + f] = hidden[f, mine]

    weights[2].wait()
    weights[3].wait()
    for f in range(frames_dev):
        for step in range(1, frame_size):
            frame_arrival(f, step).wait_recv()
    renormed = normalize(gathered[...].reshape(size, width))
    for part, target in ((0, tquery), (1, tkeys), (2, tvalues)):
        projected = jnp.dot(
            renormed, tqkv[:, part * width : (part + 1) * width], preferred_element_type=F32
        ).astype(BF16)
        if part == 2:
            target[...] = projected
        else:
            for pair in range(heads):
                span = slice(pair * PAIR, (pair + 1) * PAIR)
                piece = projected[:, span]
                turned = jnp.dot(piece, turn, preferred_element_type=F32)
                target[:, span] = (
                    piece.astype(F32) * cosine[...] + turned * sine[...]
                ).astype(BF16)

    def back_copy(step):
        peer = exclusive(slot, step, frame_size)
        return pltpu.make_async_remote_copy(
            src_ref=staged.at[peer],
            dst_ref=landed.at[:, mine],
            send_sem=back_send.at[peer],
            recv_sem=back_recv.at[slot],
            device_id=(me, peer),
            device_id_type=pl.DeviceIdType.MESH,
        )

    def back_arrival(step):
        peer = exclusive(slot, step, frame_size)
        return pltpu.make_async_remote_copy(
            src_ref=staged.at[peer],
            dst_ref=landed.at[:, pl.ds(pl.multiple_of(peer * share, 16), share)],
            send_sem=back_send.at[peer],
            recv_sem=back_recv.at[peer],
            device_id=(me, peer),
            device_id_type=pl.DeviceIdType.MESH,
        )

    def finish(turn_at, carry):
        step = frame_size - 1 - turn_at
        peer = exclusive(slot, step, frame_size)
        rows = pl.ds(pl.multiple_of(peer * chunk, 16), chunk)
        parts = []
        for pair in range(heads):
            span = slice(pair * PAIR, (pair + 1) * PAIR)
            parts.append(attend(tquery[rows, span], tkeys[:, span], tvalues[:, span], same[...]))
        time_mix = jnp.concatenate(parts, axis=1)
        before = gathered[pl.ds(peer * frames_dev, frames_dev)].reshape(chunk, width)
        after = (
            before.astype(F32) + jnp.dot(time_mix, tout[...], preferred_element_type=F32)
        ).astype(BF16)
        staged[peer] = after.reshape(frames_dev, share, width)

        @pl.when(step > 0)
        def _():
            back_copy(step).start()

        return carry

    lax.fori_loop(0, frame_size, finish, 0)
    landed[:, mine] = staged[slot]
    for step in range(1, frame_size):
        back_arrival(step).wait_recv()
    out_ref[...] = landed[...]

    for f in range(frames_dev):
        to_mate(f).wait_send()

        to_across(f).wait_send()

        @pl.when(gives_relay)
        def _():
            relay(f).wait_send()

        @pl.when(jnp.logical_or(gives_direct, gives_relayed))
        def _():
            hand_on(f).wait_send()

        for step in range(1, frame_size):
            frame_copy(f, step).wait_send()
    for step in range(1, frame_size):
        back_copy(step).wait_send()


def solution(mesh):
    res_size, frame_size = mesh.shape["res"], mesh.shape["frame"]

    def shards(activations, contacts, frame_index, spatial_qkv, spatial_out, time_qkv, time_out):
        frames_dev, block, width = activations.shape
        share = block // frame_size
        frames = frames_dev * frame_size
        size = frames * share
        vmem = pl.BlockSpec(memory_space=pltpu.VMEM)
        smem = pl.BlockSpec(memory_space=pltpu.SMEM)
        hbm = pl.BlockSpec(memory_space=pltpu.HBM)
        dma = pltpu.SemaphoreType.DMA
        return pl.pallas_call(
            functools.partial(kernel, res_size, frame_size),
            out_shape=jax.ShapeDtypeStruct((frames_dev, block, width), BF16),
            in_specs=[hbm, smem, smem, hbm, hbm, hbm, hbm],
            out_specs=vmem,
            scratch_shapes=[
                pltpu.VMEM((frames_dev, block, width), BF16),
                pltpu.VMEM(spatial_qkv.shape, BF16),
                pltpu.VMEM(spatial_out.shape, BF16),
                pltpu.VMEM(time_qkv.shape, BF16),
                pltpu.VMEM(time_out.shape, BF16),
                pltpu.VMEM((frames_dev, 5, block, width), BF16),
                pltpu.VMEM((frames_dev, block, width), BF16),
                pltpu.VMEM((frames_dev, 5 * block, width), BF16),
                pltpu.VMEM((frames_dev, 5 * block, width), BF16),
                pltpu.VMEM((block, width), BF16),
                pltpu.VMEM((frames_dev, block, width), BF16),
                pltpu.VMEM((frames, share, width), BF16),
                pltpu.VMEM((frame_size, frames_dev, share, width), BF16),
                pltpu.VMEM((frames_dev, block, width), BF16),
                pltpu.VMEM((size, width), BF16),
                pltpu.VMEM((size, width), BF16),
                pltpu.VMEM((size, width), BF16),
                pltpu.VMEM((size, PAIR), F32),
                pltpu.VMEM((size, PAIR), F32),
                pltpu.VMEM((2 * frames_dev * share, size), F32),
                dma((5,)),
                dma((frames_dev, 5)),
                dma((frames_dev, 5)),
                dma((frames_dev, frame_size)),
                dma((frames_dev, frame_size)),
                dma((frame_size,)),
                dma((frame_size,)),
            ],
            compiler_params=pltpu.CompilerParams(
                collective_id=0, has_side_effects=True, vmem_limit_bytes=56 * 1024 * 1024
            ),
        )(activations, contacts, frame_index, spatial_qkv, spatial_out, time_qkv, time_out)

    placed = (P("frame", "res", None), P(), P(), P(), P(), P(), P())
    return jax.shard_map(
        shards, mesh=mesh, in_specs=placed, out_specs=P("frame", "res", None), check_vma=False
    )
```

```python
import functools
import math

import jax
import jax.numpy as jnp
from jax import lax
from jax.experimental import pallas as pl
from jax.experimental.pallas import tpu as pltpu
from jax.sharding import PartitionSpec as P

HEAD = 64
HALO = 2
PAIR = 2 * HEAD
OWN, NEAR, DIRECT, RELAYED, FAR = range(5)
F32 = jnp.float32
BF16 = jnp.bfloat16


def exclusive(first, second, size):
    bits = [1 << i for i in range(size.bit_length() - 1)]
    return sum(((first // w + second // w) % 2) * w for w in bits)


def normalize(values_in):
    widened = values_in.astype(F32)
    mean_square = jnp.mean(widened * widened, axis=-1, keepdims=True)
    return (widened * lax.rsqrt(mean_square + 1e-06)).astype(BF16)


def attend(query, keys, values, bias):
    rows = query.shape[0]
    lanes = lax.broadcasted_iota(jnp.int32, (1, PAIR), 1)
    first = jnp.where(lanes < HEAD, HEAD ** (-0.5), 0.0).astype(BF16)
    second = jnp.where(lanes < HEAD, 0.0, HEAD ** (-0.5)).astype(BF16)
    both = jnp.concatenate([query * first, query * second], axis=0)
    scores = (
        lax.dot_general(both, keys, (((1,), (1,)), ((), ())), preferred_element_type=F32) + bias
    )
    top = jnp.max(scores, axis=-1, keepdims=True)
    expo = jnp.exp(scores - top).astype(BF16)
    wide = jnp.concatenate([values, jnp.ones_like(values)], axis=1)
    mixed = jnp.dot(expo, wide, preferred_element_type=F32)
    low = lax.broadcasted_iota(jnp.int32, (rows, PAIR), 1) < HEAD
    total = jnp.where(low, mixed[:rows, :PAIR], mixed[rows:, :PAIR])
    count = jnp.where(low, mixed[:rows, PAIR:], mixed[rows:, PAIR:])
    return (total / count).astype(BF16)


def kernel(
    res_size, frame_size,
    acts_in, contacts, frame_index, sqkv_in, sout_in, tqkv_in, tout_in, out_ref,
    acts, sqkv, sout, tqkv, tout, near, query, keys, values, mix, hidden, gathered, staged, landed,
    tquery, tkeys, tvalues, cosine, sine, same,
    weight_sem, halo_send, halo_recv, frame_send, frame_recv, back_send, back_recv,
):
    frames_dev, block, width = acts.shape
    heads = width // PAIR
    parts, share, halves = gathered.shape[0], gathered.shape[2], halo_send.shape[2]
    frames = frames_dev * frame_size
    chunk = frames_dev * share
    me = lax.axis_index("res")
    slot = lax.axis_index("frame")
    odd = lax.rem(me, 2)
    side = lax.rem(me // 2, 2)
    mate = me + 1 - 2 * odd
    across = me + 2 - 4 * side
    relay_target = me + 4 - 8 * side
    relay_source = me - 4 + 8 * side
    gives_relay = jnp.logical_and(relay_target >= 0, relay_target < res_size)
    has_relayed = jnp.logical_and(relay_source >= 0, relay_source < res_size)
    gives_direct = side == odd
    gives_relayed = jnp.logical_and(side != odd, has_relayed)
    has_far = jnp.logical_or(side != odd, has_relayed)

    weights = [
        pltpu.make_async_copy(source, target, weight_sem.at[i])
        for i, (source, target) in enumerate(
            [(sqkv_in, sqkv), (sout_in, sout), (tqkv_in, tqkv), (tout_in, tout)]
        )
    ]
    fetch = pltpu.make_async_copy(acts_in, acts, weight_sem.at[4])
    fetch.start()
    for copy in weights:
        copy.start()

    barrier = pltpu.get_barrier_semaphore()

    def greet(res, frame):
        pl.semaphore_signal(
            barrier, inc=1, device_id=(res, frame), device_id_type=pl.DeviceIdType.MESH
        )

    greet(mate, slot)
    greet(across, slot)

    @pl.when(gives_relay)
    def _():
        greet(relay_target, slot)

    @pl.when(has_relayed)
    def _():
        greet(relay_source, slot)

    for step in range(1, frame_size):
        greet(me, exclusive(slot, step, frame_size))

    fetch.wait()
    for f in range(frames_dev):
        near[f, OWN] = normalize(acts[f])

    pl.semaphore_wait(
        barrier, frame_size + 1 + gives_relay.astype(jnp.int32) + has_relayed.astype(jnp.int32)
    )

    def halo(f, half, source, target, place):
        rows = pl.ds(half * (block // halves), block // halves)
        return pltpu.make_async_remote_copy(
            src_ref=near.at[f, source, rows],
            dst_ref=near.at[f, place, rows],
            send_sem=halo_send.at[f, place, half],
            recv_sem=halo_recv.at[f, place, half],
            device_id=(target, slot),
            device_id_type=pl.DeviceIdType.MESH,
        )

    def to_mate(f, half):
        return halo(f, half, OWN, mate, NEAR)

    def to_across(f, half):
        return halo(f, half, OWN, across, DIRECT)

    def relay(f, half):
        return halo(f, half, DIRECT, relay_target, RELAYED)

    def hand_on(f, half):
        return halo(f, half, DIRECT + side + odd - 2 * side * odd, mate, FAR)

    for f in range(frames_dev):
        for half in range(halves):
            to_across(f, half).start()
            to_mate(f, half).start()

    for place, there in ((RELAYED, has_relayed), (FAR, has_far)):

        @pl.when(jnp.logical_not(there))
        def _():
            near[:, place] = jnp.zeros((frames_dev, block, width), BF16)

    size = frames * share
    lane = lax.broadcasted_iota(jnp.int32, (frames, PAIR), 1)
    row = lax.broadcasted_iota(jnp.int32, (frames, PAIR), 0)
    frequency = jnp.exp((lane & (HEAD // 2 - 1)).astype(F32) * (-math.log(10000.0) / (HEAD // 2)))
    position = jnp.zeros((frames, PAIR), F32)
    for g in range(frames):
        position = jnp.where(row == g, frame_index[g].astype(F32), position)
    angle = position * frequency
    for table, entries in ((cosine, jnp.cos(angle)), (sine, jnp.sin(angle))):
        table[...] = jnp.broadcast_to(entries[:, None, :], (frames, share, PAIR)).reshape(
            size, PAIR
        )
    row = lax.broadcasted_iota(jnp.int32, same.shape, 0)
    column = lax.broadcasted_iota(jnp.int32, same.shape, 1)
    same[...] = jnp.where((row & (share - 1)) == (column & (share - 1)), 0.0, -1e30)
    row = lax.broadcasted_iota(jnp.int32, (PAIR, PAIR), 0)
    column = lax.broadcasted_iota(jnp.int32, (PAIR, PAIR), 1)
    upper = (column & (HEAD - 1)) >= HEAD // 2
    turn = jnp.where(
        upper,
        jnp.where(row == column - HEAD // 2, 1.0, 0.0),
        jnp.where(row == column + HEAD // 2, -1.0, 0.0),
    ).astype(BF16)
    order = (HALO, 3 - 2 * odd, 2 * HALO * (1 - side), 2 * HALO * side, 1 + 2 * odd)
    bias = jnp.concatenate(
        [
            jnp.full((1, block), jnp.where(contacts[me, place] > 0, 0.0, -1e30), F32)
            for place in order
        ],
        axis=1,
    )

    def project(f, first, count):
        rows = near[f, first : first + count].reshape(count * block, width)
        span = slice(first * block, (first + count) * block)
        for part, target in ((1, keys), (2, values)):
            target[f, span] = jnp.dot(
                rows, sqkv[:, part * width : (part + 1) * width], preferred_element_type=F32
            ).astype(BF16)

    def pass_on(f, half):
        to_across(f, half).wait_recv()

        @pl.when(gives_relay)
        def _():
            relay(f, half).start()

        @pl.when(gives_direct)
        def _():
            hand_on(f, half).start()

    def take_relayed(f):
        for half in range(halves):

            @pl.when(has_relayed)
            def _():
                relay(f, half).wait_recv()

            @pl.when(gives_relayed)
            def _():
                hand_on(f, half).start()

        project(f, RELAYED, 1)

    def take_far(f):
        @pl.when(has_far)
        def _():
            for half in range(halves):
                hand_on(f, half).wait_recv()

        project(f, FAR, 1)

    def frame_copy(f, part, step):
        peer = exclusive(slot, step, frame_size)
        first = part * (block // parts) + peer * share
        return pltpu.make_async_remote_copy(
            src_ref=hidden.at[f, pl.ds(pl.multiple_of(first, 16), share)],
            dst_ref=gathered.at[part, slot * frames_dev + f],
            send_sem=frame_send.at[f, part, peer],
            recv_sem=frame_recv.at[f, part, slot],
            device_id=(me, peer),
            device_id_type=pl.DeviceIdType.MESH,
        )

    def frame_arrival(f, part, step):
        peer = exclusive(slot, step, frame_size)
        return pltpu.make_async_remote_copy(
            src_ref=hidden.at[f, pl.ds(0, share)],
            dst_ref=gathered.at[part, peer * frames_dev + f],
            send_sem=frame_send.at[f, part, peer],
            recv_sem=frame_recv.at[f, part, peer],
            device_id=(me, peer),
            device_id_type=pl.DeviceIdType.MESH,
        )

    def spatial(f, first, count):
        rows = slice(first * (block // parts), (first + count) * (block // parts))
        for pair in range(heads):
            span = slice(pair * PAIR, (pair + 1) * PAIR)
            mix[rows, span] = attend(
                query[f, rows, span], keys[f, :, span], values[f, :, span], bias
            )
        hidden[f, rows] = (
            acts[f, rows].astype(F32)
            + jnp.dot(mix[rows], sout[...], preferred_element_type=F32)
        ).astype(BF16)
        for part in range(first, first + count):
            for step in range(frame_size - 1, 0, -1):
                frame_copy(f, part, step).start()
            mine = pl.ds(pl.multiple_of(part * (block // parts) + slot * share, 16), share)
            gathered[part, slot * frames_dev + f] = hidden[f, mine]

    weights[0].wait()
    for f in range(frames_dev):
        query[f] = jnp.dot(near[f, OWN], sqkv[:, :width], preferred_element_type=F32).astype(BF16)
        for half in range(halves):
            to_mate(f, half).wait_recv()
        project(f, OWN, 2)
        pass_on(0, f)
    project(0, DIRECT, 1)
    pass_on(1, 0)
    take_relayed(0)
    pass_on(1, 1)
    take_far(0)
    weights[1].wait()
    spatial(0, 0, parts)
    project(1, DIRECT, 1)
    take_relayed(1)
    take_far(1)
    for part in range(parts):
        spatial(1, part, 1)

    def back_copy(part, peer):
        first = part * (block // parts) + slot * share
        return pltpu.make_async_remote_copy(
            src_ref=staged.at[part, peer],
            dst_ref=landed.at[:, pl.ds(pl.multiple_of(first, 16), share)],
            send_sem=back_send.at[part, peer],
            recv_sem=back_recv.at[part, slot],
            device_id=(me, peer),
            device_id_type=pl.DeviceIdType.MESH,
        )

    def back_arrival(part, peer):
        first = part * (block // parts) + peer * share
        return pltpu.make_async_remote_copy(
            src_ref=staged.at[part, peer],
            dst_ref=landed.at[:, pl.ds(pl.multiple_of(first, 16), share)],
            send_sem=back_send.at[part, peer],
            recv_sem=back_recv.at[part, peer],
            device_id=(me, peer),
            device_id_type=pl.DeviceIdType.MESH,
        )

    weights[2].wait()
    weights[3].wait()
    for part in range(parts):
        for f in range(frames_dev):
            for step in range(1, frame_size):
                frame_arrival(f, part, step).wait_recv()
        renormed = normalize(gathered[part].reshape(size, width))
        for third, target in ((0, tquery), (1, tkeys), (2, tvalues)):
            projected = jnp.dot(
                renormed, tqkv[:, third * width : (third + 1) * width], preferred_element_type=F32
            ).astype(BF16)
            if third == 2:
                target[...] = projected
            else:
                for pair in range(heads):
                    span = slice(pair * PAIR, (pair + 1) * PAIR)
                    piece = projected[:, span]
                    turned = jnp.dot(piece, turn, preferred_element_type=F32)
                    target[:, span] = (
                        piece.astype(F32) * cosine[...] + turned * sine[...]
                    ).astype(BF16)
        for apart in range(frame_size // 2 - 1, -1, -1):
            first = 2 * exclusive(slot // 2, apart, frame_size // 2)
            rows = pl.ds(pl.multiple_of(first * chunk, 16), 2 * chunk)
            pieces = []
            for pair in range(heads):
                span = slice(pair * PAIR, (pair + 1) * PAIR)
                pieces.append(
                    attend(tquery[rows, span], tkeys[:, span], tvalues[:, span], same[...])
                )
            time_mix = jnp.concatenate(pieces, axis=1)
            before = gathered[part, pl.ds(first * frames_dev, 2 * frames_dev)]
            after = (
                before.reshape(2 * chunk, width).astype(F32)
                + jnp.dot(time_mix, tout[...], preferred_element_type=F32)
            ).astype(BF16)
            staged[part, pl.ds(first, 2)] = after.reshape(2, frames_dev, share, width)
            if apart > 0:
                back_copy(part, first).start()
                back_copy(part, first + 1).start()
            else:
                back_copy(part, first + 1 - slot % 2).start()
                mine = pl.ds(pl.multiple_of(part * (block // parts) + slot * share, 16), share)
                landed[:, mine] = staged[part, slot]

    for part in range(parts):
        for step in range(1, frame_size):
            back_arrival(part, exclusive(slot, step, frame_size)).wait_recv()
    out_ref[...] = landed[...]

    for f in range(frames_dev):
        for half in range(halves):
            to_mate(f, half).wait_send()
            to_across(f, half).wait_send()

            @pl.when(gives_relay)
            def _():
                relay(f, half).wait_send()

            @pl.when(jnp.logical_or(gives_direct, gives_relayed))
            def _():
                hand_on(f, half).wait_send()

        for part in range(parts):
            for step in range(1, frame_size):
                frame_copy(f, part, step).wait_send()
    for part in range(parts):
        for step in range(1, frame_size):
            back_copy(part, exclusive(slot, step, frame_size)).wait_send()


def solution(mesh):
    res_size, frame_size = mesh.shape["res"], mesh.shape["frame"]

    def shards(activations, contacts, frame_index, spatial_qkv, spatial_out, time_qkv, time_out):
        frames_dev, block, width = activations.shape
        share = 16
        parts = block // (frame_size * share)
        frames = frames_dev * frame_size
        size = frames * share
        vmem = pl.BlockSpec(memory_space=pltpu.VMEM)
        smem = pl.BlockSpec(memory_space=pltpu.SMEM)
        hbm = pl.BlockSpec(memory_space=pltpu.HBM)
        dma = pltpu.SemaphoreType.DMA
        return pl.pallas_call(
            functools.partial(kernel, res_size, frame_size),
            out_shape=jax.ShapeDtypeStruct((frames_dev, block, width), BF16),
            in_specs=[hbm, smem, smem, hbm, hbm, hbm, hbm],
            out_specs=vmem,
            scratch_shapes=[
                pltpu.VMEM((frames_dev, block, width), BF16),
                pltpu.VMEM(spatial_qkv.shape, BF16),
                pltpu.VMEM(spatial_out.shape, BF16),
                pltpu.VMEM(time_qkv.shape, BF16),
                pltpu.VMEM(time_out.shape, BF16),
                pltpu.VMEM((frames_dev, 5, block, width), BF16),
                pltpu.VMEM((frames_dev, block, width), BF16),
                pltpu.VMEM((frames_dev, 5 * block, width), BF16),
                pltpu.VMEM((frames_dev, 5 * block, width), BF16),
                pltpu.VMEM((block, width), BF16),
                pltpu.VMEM((frames_dev, block, width), BF16),
                pltpu.VMEM((parts, frames, share, width), BF16),
                pltpu.VMEM((parts, frame_size, frames_dev, share, width), BF16),
                pltpu.VMEM((frames_dev, block, width), BF16),
                pltpu.VMEM((size, width), BF16),
                pltpu.VMEM((size, width), BF16),
                pltpu.VMEM((size, width), BF16),
                pltpu.VMEM((size, PAIR), F32),
                pltpu.VMEM((size, PAIR), F32),
                pltpu.VMEM((4 * frames_dev * share, size), F32),
                dma((5,)),
                dma((frames_dev, 5, 2)),
                dma((frames_dev, 5, 2)),
                dma((frames_dev, parts, frame_size)),
                dma((frames_dev, parts, frame_size)),
                dma((parts, frame_size)),
                dma((parts, frame_size)),
            ],
            compiler_params=pltpu.CompilerParams(
                collective_id=0, has_side_effects=True, vmem_limit_bytes=53 * 1024 * 1024
            ),
        )(activations, contacts, frame_index, spatial_qkv, spatial_out, time_qkv, time_out)

    placed = (P("frame", "res", None), P(), P(), P(), P(), P(), P())
    return jax.shard_map(
        shards, mesh=mesh, in_specs=placed, out_specs=P("frame", "res", None), check_vma=False
    )
```

```python
import functools
import math

import jax
import jax.numpy as jnp
from jax import lax
from jax.experimental import pallas as pl
from jax.experimental.pallas import tpu as pltpu
from jax.sharding import PartitionSpec as P

HEAD = 64
HALO = 2
PAIR = 2 * HEAD
OWN, NEAR, DIRECT, RELAYED, FAR = range(5)
F32 = jnp.float32
BF16 = jnp.bfloat16


def exclusive(first, second, size):
    bits = [1 << i for i in range(size.bit_length() - 1)]
    return sum(((first // w + second // w) % 2) * w for w in bits)


def normalize(values_in):
    widened = values_in.astype(F32)
    mean_square = jnp.mean(widened * widened, axis=-1, keepdims=True)
    return (widened * lax.rsqrt(mean_square + 1e-06)).astype(BF16)


def attend(query, keys, values, bias):
    rows = query.shape[0]
    lanes = lax.broadcasted_iota(jnp.int32, (1, PAIR), 1)
    first = jnp.where(lanes < HEAD, HEAD ** (-0.5), 0.0).astype(BF16)
    second = jnp.where(lanes < HEAD, 0.0, HEAD ** (-0.5)).astype(BF16)
    both = jnp.concatenate([query * first, query * second], axis=0)
    scores = (
        lax.dot_general(both, keys, (((1,), (1,)), ((), ())), preferred_element_type=F32) + bias
    )
    top = jnp.max(scores, axis=-1, keepdims=True)
    expo = jnp.exp(scores - top).astype(BF16)
    wide = jnp.concatenate([values, jnp.ones_like(values)], axis=1)
    mixed = jnp.dot(expo, wide, preferred_element_type=F32)
    low = lax.broadcasted_iota(jnp.int32, (rows, PAIR), 1) < HEAD
    highest = jnp.where(low, top[:rows], top[rows:])
    total = jnp.where(low, mixed[:rows, :PAIR], mixed[rows:, :PAIR])
    count = jnp.where(low, mixed[:rows, PAIR:], mixed[rows:, PAIR:])
    return highest, total, count


def kernel(
    res_size, frame_size,
    acts_in, contacts, frame_index, sqkv_in, sout_in, tqkv_in, tout_in, out_ref,
    acts, sqkv, sout, tqkv, tout, near, query, keys, values, mix, hidden, gathered, staged, landed,
    tquery, tkeys, tvalues, cosine, sine, same, highest, total, count,
    weight_sem, halo_send, halo_recv, frame_send, frame_recv, back_send, back_recv,
):
    frames_dev, block, width = acts.shape
    heads = width // PAIR
    parts, share, halves = gathered.shape[0], gathered.shape[2], halo_send.shape[2]
    frames = frames_dev * frame_size
    chunk = frames_dev * share
    me = lax.axis_index("res")
    slot = lax.axis_index("frame")
    odd = lax.rem(me, 2)
    side = lax.rem(me // 2, 2)
    mate = me + 1 - 2 * odd
    across = me + 2 - 4 * side
    relay_target = me + 4 - 8 * side
    relay_source = me - 4 + 8 * side
    gives_relay = jnp.logical_and(relay_target >= 0, relay_target < res_size)
    has_relayed = jnp.logical_and(relay_source >= 0, relay_source < res_size)
    gives_direct = side == odd
    gives_relayed = jnp.logical_and(side != odd, has_relayed)
    has_far = jnp.logical_or(side != odd, has_relayed)

    weights = [
        pltpu.make_async_copy(source, target, weight_sem.at[i])
        for i, (source, target) in enumerate(
            [(sqkv_in, sqkv), (sout_in, sout), (tqkv_in, tqkv), (tout_in, tout)]
        )
    ]
    fetch = pltpu.make_async_copy(acts_in, acts, weight_sem.at[4])
    fetch.start()
    for copy in weights:
        copy.start()

    barrier = pltpu.get_barrier_semaphore()

    def greet(res, frame):
        pl.semaphore_signal(
            barrier, inc=1, device_id=(res, frame), device_id_type=pl.DeviceIdType.MESH
        )

    greet(mate, slot)
    greet(across, slot)

    @pl.when(gives_relay)
    def _():
        greet(relay_target, slot)

    @pl.when(has_relayed)
    def _():
        greet(relay_source, slot)

    for step in range(1, frame_size):
        greet(me, exclusive(slot, step, frame_size))

    fetch.wait()
    for f in range(frames_dev):
        near[f, OWN] = normalize(acts[f])

    pl.semaphore_wait(
        barrier, frame_size + 1 + gives_relay.astype(jnp.int32) + has_relayed.astype(jnp.int32)
    )

    def halo(f, half, source, target, place):
        rows = pl.ds(half * (block // halves), block // halves)
        return pltpu.make_async_remote_copy(
            src_ref=near.at[f, source, rows],
            dst_ref=near.at[f, place, rows],
            send_sem=halo_send.at[f, place, half],
            recv_sem=halo_recv.at[f, place, half],
            device_id=(target, slot),
            device_id_type=pl.DeviceIdType.MESH,
        )

    def to_mate(f, half):
        return halo(f, half, OWN, mate, NEAR)

    def to_across(f, half):
        return halo(f, half, OWN, across, DIRECT)

    def relay(f, half):
        return halo(f, half, DIRECT, relay_target, RELAYED)

    def hand_on(f, half):
        return halo(f, half, DIRECT + side + odd - 2 * side * odd, mate, FAR)

    for f in range(frames_dev):
        for half in range(halves):
            to_across(f, half).start()
            to_mate(f, half).start()

    for place, there in ((RELAYED, has_relayed), (FAR, has_far)):

        @pl.when(jnp.logical_not(there))
        def _():
            for target in (keys, values):
                target[:, place * block : (place + 1) * block] = jnp.zeros(
                    (frames_dev, block, width), BF16
                )

    size = frames * share
    lane = lax.broadcasted_iota(jnp.int32, (frames, PAIR), 1)
    row = lax.broadcasted_iota(jnp.int32, (frames, PAIR), 0)
    frequency = jnp.exp((lane & (HEAD // 2 - 1)).astype(F32) * (-math.log(10000.0) / (HEAD // 2)))
    position = jnp.zeros((frames, PAIR), F32)
    for g in range(frames):
        position = jnp.where(row == g, frame_index[g].astype(F32), position)
    angle = position * frequency
    for table, entries in ((cosine, jnp.cos(angle)), (sine, jnp.sin(angle))):
        table[...] = jnp.broadcast_to(entries[:, None, :], (frames, share, PAIR)).reshape(
            size, PAIR
        )
    row = lax.broadcasted_iota(jnp.int32, same.shape, 0)
    column = lax.broadcasted_iota(jnp.int32, same.shape, 1)
    same[...] = jnp.where((row & (share - 1)) == (column & (share - 1)), 0.0, -1e30)
    row = lax.broadcasted_iota(jnp.int32, (PAIR, PAIR), 0)
    column = lax.broadcasted_iota(jnp.int32, (PAIR, PAIR), 1)
    upper = (column & (HEAD - 1)) >= HEAD // 2
    turn = jnp.where(
        upper,
        jnp.where(row == column - HEAD // 2, 1.0, 0.0),
        jnp.where(row == column + HEAD // 2, -1.0, 0.0),
    ).astype(BF16)
    order = (HALO, 3 - 2 * odd, 2 * HALO * (1 - side), 2 * HALO * side, 1 + 2 * odd)
    bias = jnp.concatenate(
        [
            jnp.full((1, block), jnp.where(contacts[me, place] > 0, 0.0, -1e30), F32)
            for place in order
        ],
        axis=1,
    )

    def project(f, first, count):
        rows = near[f, first : first + count].reshape(count * block, width)
        span = slice(first * block, (first + count) * block)
        for part, target in ((1, keys), (2, values)):
            target[f, span] = jnp.dot(
                rows, sqkv[:, part * width : (part + 1) * width], preferred_element_type=F32
            ).astype(BF16)

    def pass_on(f, half):
        to_across(f, half).wait_recv()

        @pl.when(gives_relay)
        def _():
            relay(f, half).start()

        @pl.when(gives_direct)
        def _():
            hand_on(f, half).start()

    def take_relayed(f):
        for half in range(halves):

            @pl.when(has_relayed)
            def _():
                relay(f, half).wait_recv()

            @pl.when(gives_relayed)
            def _():
                hand_on(f, half).start()

        @pl.when(has_relayed)
        def _():
            project(f, RELAYED, 1)

    def take_far(f):
        @pl.when(has_far)
        def _():
            for half in range(halves):
                hand_on(f, half).wait_recv()
            project(f, FAR, 1)

    def frame_copy(f, part, step):
        peer = exclusive(slot, step, frame_size)
        first = part * (block // parts) + peer * share
        return pltpu.make_async_remote_copy(
            src_ref=hidden.at[f, pl.ds(pl.multiple_of(first, 16), share)],
            dst_ref=gathered.at[part, slot * frames_dev + f],
            send_sem=frame_send.at[f, part, peer],
            recv_sem=frame_recv.at[f, part, slot],
            device_id=(me, peer),
            device_id_type=pl.DeviceIdType.MESH,
        )

    def frame_arrival(f, part, step):
        peer = exclusive(slot, step, frame_size)
        return pltpu.make_async_remote_copy(
            src_ref=hidden.at[f, pl.ds(0, share)],
            dst_ref=gathered.at[part, peer * frames_dev + f],
            send_sem=frame_send.at[f, part, peer],
            recv_sem=frame_recv.at[f, part, peer],
            device_id=(me, peer),
            device_id_type=pl.DeviceIdType.MESH,
        )

    split = RELAYED * block

    def begin(f):
        for pair in range(heads):
            span = slice(pair * PAIR, (pair + 1) * PAIR)
            highest[:, span], total[:, span], count[:, span] = attend(
                query[f, :, span],
                keys[f, :split, span],
                values[f, :split, span],
                bias[:, :split],
            )

    def spatial(f, first, many):
        rows = slice(first * (block // parts), (first + many) * (block // parts))
        for pair in range(heads):
            span = slice(pair * PAIR, (pair + 1) * PAIR)
            top, more, extra = attend(
                query[f, rows, span],
                keys[f, split:, span],
                values[f, split:, span],
                bias[:, split:],
            )
            peak = jnp.maximum(highest[rows, span], top)
            old, new = jnp.exp(highest[rows, span] - peak), jnp.exp(top - peak)
            mix[rows, span] = (
                (total[rows, span] * old + more * new) / (count[rows, span] * old + extra * new)
            ).astype(BF16)
        hidden[f, rows] = (
            acts[f, rows].astype(F32)
            + jnp.dot(mix[rows], sout[...], preferred_element_type=F32)
        ).astype(BF16)
        for part in range(first, first + many):
            for step in range(frame_size - 1, 0, -1):
                frame_copy(f, part, step).start()
            mine = pl.ds(pl.multiple_of(part * (block // parts) + slot * share, 16), share)
            gathered[part, slot * frames_dev + f] = hidden[f, mine]

    weights[0].wait()
    for f in range(frames_dev):
        query[f] = jnp.dot(near[f, OWN], sqkv[:, :width], preferred_element_type=F32).astype(BF16)
        for half in range(halves):
            to_mate(f, half).wait_recv()
        project(f, OWN, 2)
        pass_on(0, f)
    project(0, DIRECT, 1)
    begin(0)
    pass_on(1, 0)
    take_relayed(0)
    pass_on(1, 1)
    take_far(0)
    weights[1].wait()
    spatial(0, 0, parts)
    project(1, DIRECT, 1)
    begin(1)
    take_relayed(1)
    take_far(1)
    for part in range(parts):
        spatial(1, part, 1)

    def back_copy(part, peer):
        first = part * (block // parts) + slot * share
        return pltpu.make_async_remote_copy(
            src_ref=staged.at[part, peer],
            dst_ref=landed.at[:, pl.ds(pl.multiple_of(first, 16), share)],
            send_sem=back_send.at[part, peer],
            recv_sem=back_recv.at[part, slot],
            device_id=(me, peer),
            device_id_type=pl.DeviceIdType.MESH,
        )

    def back_arrival(part, peer):
        first = part * (block // parts) + peer * share
        return pltpu.make_async_remote_copy(
            src_ref=staged.at[part, peer],
            dst_ref=landed.at[:, pl.ds(pl.multiple_of(first, 16), share)],
            send_sem=back_send.at[part, peer],
            recv_sem=back_recv.at[part, peer],
            device_id=(me, peer),
            device_id_type=pl.DeviceIdType.MESH,
        )

    weights[2].wait()
    weights[3].wait()
    for part in range(parts):
        for f in range(frames_dev):
            for step in range(1, frame_size):
                frame_arrival(f, part, step).wait_recv()
        renormed = normalize(gathered[part].reshape(size, width))
        for third, target in ((0, tquery), (1, tkeys), (2, tvalues)):
            projected = jnp.dot(
                renormed, tqkv[:, third * width : (third + 1) * width], preferred_element_type=F32
            ).astype(BF16)
            if third == 2:
                target[...] = projected
            else:
                for pair in range(heads):
                    span = slice(pair * PAIR, (pair + 1) * PAIR)
                    piece = projected[:, span]
                    turned = jnp.dot(piece, turn, preferred_element_type=F32)
                    target[:, span] = (
                        piece.astype(F32) * cosine[...] + turned * sine[...]
                    ).astype(BF16)
        for apart in range(frame_size // 2 - 1, -1, -1):
            first = 2 * exclusive(slot // 2, apart, frame_size // 2)
            rows = pl.ds(pl.multiple_of(first * chunk, 16), 2 * chunk)
            pieces = []
            for pair in range(heads):
                span = slice(pair * PAIR, (pair + 1) * PAIR)
                _, time_total, time_count = attend(
                    tquery[rows, span], tkeys[:, span], tvalues[:, span], same[...]
                )
                pieces.append((time_total / time_count).astype(BF16))
            time_mix = jnp.concatenate(pieces, axis=1)
            before = gathered[part, pl.ds(first * frames_dev, 2 * frames_dev)]
            after = (
                before.reshape(2 * chunk, width).astype(F32)
                + jnp.dot(time_mix, tout[...], preferred_element_type=F32)
            ).astype(BF16)
            staged[part, pl.ds(first, 2)] = after.reshape(2, frames_dev, share, width)
            if apart > 0:
                back_copy(part, first).start()
                back_copy(part, first + 1).start()
            else:
                back_copy(part, first + 1 - slot % 2).start()
                mine = pl.ds(pl.multiple_of(part * (block // parts) + slot * share, 16), share)
                landed[:, mine] = staged[part, slot]

    for part in range(parts):
        for step in range(1, frame_size):
            back_arrival(part, exclusive(slot, step, frame_size)).wait_recv()
    out_ref[...] = landed[...]

    for f in range(frames_dev):
        for half in range(halves):
            to_mate(f, half).wait_send()
            to_across(f, half).wait_send()

            @pl.when(gives_relay)
            def _():
                relay(f, half).wait_send()

            @pl.when(jnp.logical_or(gives_direct, gives_relayed))
            def _():
                hand_on(f, half).wait_send()

        for part in range(parts):
            for step in range(1, frame_size):
                frame_copy(f, part, step).wait_send()
    for part in range(parts):
        for step in range(1, frame_size):
            back_copy(part, exclusive(slot, step, frame_size)).wait_send()


def solution(mesh):
    res_size, frame_size = mesh.shape["res"], mesh.shape["frame"]

    def shards(activations, contacts, frame_index, spatial_qkv, spatial_out, time_qkv, time_out):
        frames_dev, block, width = activations.shape
        share = 16
        parts = block // (frame_size * share)
        frames = frames_dev * frame_size
        size = frames * share
        vmem = pl.BlockSpec(memory_space=pltpu.VMEM)
        smem = pl.BlockSpec(memory_space=pltpu.SMEM)
        hbm = pl.BlockSpec(memory_space=pltpu.HBM)
        dma = pltpu.SemaphoreType.DMA
        return pl.pallas_call(
            functools.partial(kernel, res_size, frame_size),
            out_shape=jax.ShapeDtypeStruct((frames_dev, block, width), BF16),
            in_specs=[hbm, smem, smem, hbm, hbm, hbm, hbm],
            out_specs=vmem,
            scratch_shapes=[
                pltpu.VMEM((frames_dev, block, width), BF16),
                pltpu.VMEM(spatial_qkv.shape, BF16),
                pltpu.VMEM(spatial_out.shape, BF16),
                pltpu.VMEM(time_qkv.shape, BF16),
                pltpu.VMEM(time_out.shape, BF16),
                pltpu.VMEM((frames_dev, 5, block, width), BF16),
                pltpu.VMEM((frames_dev, block, width), BF16),
                pltpu.VMEM((frames_dev, 5 * block, width), BF16),
                pltpu.VMEM((frames_dev, 5 * block, width), BF16),
                pltpu.VMEM((block, width), BF16),
                pltpu.VMEM((frames_dev, block, width), BF16),
                pltpu.VMEM((parts, frames, share, width), BF16),
                pltpu.VMEM((parts, frame_size, frames_dev, share, width), BF16),
                pltpu.VMEM((frames_dev, block, width), BF16),
                pltpu.VMEM((size, width), BF16),
                pltpu.VMEM((size, width), BF16),
                pltpu.VMEM((size, width), BF16),
                pltpu.VMEM((size, PAIR), F32),
                pltpu.VMEM((size, PAIR), F32),
                pltpu.VMEM((4 * frames_dev * share, size), F32),
                pltpu.VMEM((block, width), F32),
                pltpu.VMEM((block, width), F32),
                pltpu.VMEM((block, width), F32),
                dma((5,)),
                dma((frames_dev, 5, 2)),
                dma((frames_dev, 5, 2)),
                dma((frames_dev, parts, frame_size)),
                dma((frames_dev, parts, frame_size)),
                dma((parts, frame_size)),
                dma((parts, frame_size)),
            ],
            compiler_params=pltpu.CompilerParams(
                collective_id=0, has_side_effects=True, vmem_limit_bytes=56 * 1024 * 1024
            ),
        )(activations, contacts, frame_index, spatial_qkv, spatial_out, time_qkv, time_out)

    placed = (P("frame", "res", None), P(), P(), P(), P(), P(), P())
    return jax.shard_map(
        shards, mesh=mesh, in_specs=placed, out_specs=P("frame", "res", None), check_vma=False
    )
```

```python
import functools
import math

import jax
import jax.numpy as jnp
from jax import lax
from jax.experimental import pallas as pl
from jax.experimental.pallas import tpu as pltpu
from jax.sharding import PartitionSpec as P

HEAD = 64
HALO = 2
PAIR = 2 * HEAD
OWN, NEAR, DIRECT, RELAYED, FAR = range(5)
F32 = jnp.float32
BF16 = jnp.bfloat16


def exclusive(first, second, size):
    bits = [1 << i for i in range(size.bit_length() - 1)]
    return sum(((first // w + second // w) % 2) * w for w in bits)


def normalize(values_in):
    widened = values_in.astype(F32)
    mean_square = jnp.mean(widened * widened, axis=-1, keepdims=True)
    return (widened * lax.rsqrt(mean_square + 1e-06)).astype(BF16)


def attend(query, keys, values, bias):
    rows = query.shape[0]
    lanes = lax.broadcasted_iota(jnp.int32, (1, PAIR), 1)
    first = jnp.where(lanes < HEAD, HEAD ** (-0.5), 0.0).astype(BF16)
    second = jnp.where(lanes < HEAD, 0.0, HEAD ** (-0.5)).astype(BF16)
    both = jnp.concatenate([query * first, query * second], axis=0)
    scores = (
        lax.dot_general(both, keys, (((1,), (1,)), ((), ())), preferred_element_type=F32) + bias
    )
    top = jnp.max(scores, axis=-1, keepdims=True)
    expo = jnp.exp(scores - top).astype(BF16)
    wide = jnp.concatenate([values, jnp.ones_like(values)], axis=1)
    mixed = jnp.dot(expo, wide, preferred_element_type=F32)
    low = lax.broadcasted_iota(jnp.int32, (rows, PAIR), 1) < HEAD
    highest = jnp.where(low, top[:rows], top[rows:])
    total = jnp.where(low, mixed[:rows, :PAIR], mixed[rows:, :PAIR])
    count = jnp.where(low, mixed[:rows, PAIR:], mixed[rows:, PAIR:])
    return highest, total, count


def kernel(
    res_size, frame_size,
    acts_in, contacts, frame_index, sqkv_in, sout_in, tqkv_in, tout_in, out_ref,
    acts, sqkv, sout, tqkv, tout, near, query, keys, values, mix, hidden, gathered, staged, landed,
    tquery, tkeys, tvalues, cosine, sine, same, highest, total, count,
    weight_sem, halo_send, halo_recv, frame_send, frame_recv, back_send, back_recv,
):
    frames_dev, block, width = acts.shape
    heads = width // PAIR
    parts, share, halves = gathered.shape[1], gathered.shape[3], halo_send.shape[2]
    frames = frames_dev * frame_size
    chunk = frames_dev * share
    me = lax.axis_index("res")
    slot = lax.axis_index("frame")
    odd = lax.rem(me, 2)
    side = lax.rem(me // 2, 2)
    mate = me + 1 - 2 * odd
    across = me + 2 - 4 * side
    relay_target = me + 4 - 8 * side
    relay_source = me - 4 + 8 * side
    gives_relay = jnp.logical_and(relay_target >= 0, relay_target < res_size)
    has_relayed = jnp.logical_and(relay_source >= 0, relay_source < res_size)
    gives_direct = side == odd
    gives_relayed = jnp.logical_and(side != odd, has_relayed)
    has_far = jnp.logical_or(side != odd, has_relayed)

    weights = [
        pltpu.make_async_copy(source, target, weight_sem.at[i])
        for i, (source, target) in enumerate(
            [(sqkv_in, sqkv), (sout_in, sout), (tqkv_in, tqkv), (tout_in, tout)]
        )
    ]
    fetch = pltpu.make_async_copy(acts_in, acts, weight_sem.at[4])
    fetch.start()
    weights[0].start()

    barrier = pltpu.get_barrier_semaphore()

    def greet(res, frame):
        pl.semaphore_signal(
            barrier, inc=1, device_id=(res, frame), device_id_type=pl.DeviceIdType.MESH
        )

    greet(mate, slot)
    greet(across, slot)

    @pl.when(gives_relay)
    def _():
        greet(relay_target, slot)

    @pl.when(has_relayed)
    def _():
        greet(relay_source, slot)

    for step in range(1, frame_size):
        greet(me, exclusive(slot, step, frame_size))

    fetch.wait()
    near[0, OWN] = normalize(acts[0])

    pl.semaphore_wait(
        barrier, frame_size + 1 + gives_relay.astype(jnp.int32) + has_relayed.astype(jnp.int32)
    )

    def halo(f, half, source, target, place):
        rows = pl.ds(half * (block // halves), block // halves)
        return pltpu.make_async_remote_copy(
            src_ref=near.at[f, source, rows],
            dst_ref=near.at[f, place, rows],
            send_sem=halo_send.at[f, place, half],
            recv_sem=halo_recv.at[f, place, half],
            device_id=(target, slot),
            device_id_type=pl.DeviceIdType.MESH,
        )

    def to_mate(f, half):
        return halo(f, half, OWN, mate, NEAR)

    def to_across(f, half):
        return halo(f, half, OWN, across, DIRECT)

    def relay(f, half):
        return halo(f, half, DIRECT, relay_target, RELAYED)

    def hand_on(f, half):
        return halo(f, half, DIRECT + side + odd - 2 * side * odd, mate, FAR)

    for f in range(frames_dev):
        if f > 0:
            near[f, OWN] = normalize(acts[f])
        for half in range(halves):
            to_across(f, half).start()
            to_mate(f, half).start()

    for place, there in ((RELAYED, has_relayed), (FAR, has_far)):

        @pl.when(jnp.logical_not(there))
        def _():
            for target in (keys, values):
                target[:, place * block : (place + 1) * block] = jnp.zeros(
                    (frames_dev, block, width), BF16
                )

    size = frames * share
    lane = lax.broadcasted_iota(jnp.int32, (frames, PAIR), 1)
    frequency = jnp.exp((lane & (HEAD // 2 - 1)).astype(F32) * (-math.log(10000.0) / (HEAD // 2)))
    position = jnp.zeros((frames, PAIR), F32)
    row = lax.broadcasted_iota(jnp.int32, (frames, PAIR), 0)
    for g in range(frames):
        at = (g % frames_dev) * frame_size + g // frames_dev
        position = jnp.where(row == at, frame_index[g].astype(F32), position)
    angle = position * frequency
    for table, entries in ((cosine, jnp.cos(angle)), (sine, jnp.sin(angle))):
        table[...] = jnp.broadcast_to(entries[:, None, :], (frames, share, PAIR)).reshape(
            size, PAIR
        )
    row = lax.broadcasted_iota(jnp.int32, same.shape, 0)
    column = lax.broadcasted_iota(jnp.int32, same.shape, 1)
    same[...] = jnp.where((row & (share - 1)) == (column & (share - 1)), 0.0, -1e30)
    row = lax.broadcasted_iota(jnp.int32, (PAIR, PAIR), 0)
    column = lax.broadcasted_iota(jnp.int32, (PAIR, PAIR), 1)
    upper = (column & (HEAD - 1)) >= HEAD // 2
    turn = jnp.where(
        upper,
        jnp.where(row == column - HEAD // 2, 1.0, 0.0),
        jnp.where(row == column + HEAD // 2, -1.0, 0.0),
    ).astype(BF16)
    order = (HALO, 3 - 2 * odd, 2 * HALO * (1 - side), 2 * HALO * side, 1 + 2 * odd)
    bias = jnp.concatenate(
        [
            jnp.full((1, block), jnp.where(contacts[me, place] > 0, 0.0, -1e30), F32)
            for place in order
        ],
        axis=1,
    )

    def project(f, first, count):
        rows = near[f, first : first + count].reshape(count * block, width)
        span = slice(first * block, (first + count) * block)
        for part, target in ((1, keys), (2, values)):
            target[f, span] = jnp.dot(
                rows, sqkv[:, part * width : (part + 1) * width], preferred_element_type=F32
            ).astype(BF16)

    def pass_on(f, half):
        to_across(f, half).wait_recv()

        @pl.when(gives_relay)
        def _():
            relay(f, half).start()

        @pl.when(gives_direct)
        def _():
            hand_on(f, half).start()

    def take_relayed(f):
        for half in range(halves):

            @pl.when(has_relayed)
            def _():
                relay(f, half).wait_recv()

            @pl.when(gives_relayed)
            def _():
                hand_on(f, half).start()

        @pl.when(has_relayed)
        def _():
            project(f, RELAYED, 1)

    def take_far(f):
        @pl.when(has_far)
        def _():
            for half in range(halves):
                hand_on(f, half).wait_recv()
            project(f, FAR, 1)

    def frame_copy(f, part, step):
        peer = exclusive(slot, step, frame_size)
        first = part * (block // parts) + peer * share
        return pltpu.make_async_remote_copy(
            src_ref=hidden.at[f, pl.ds(pl.multiple_of(first, 16), share)],
            dst_ref=gathered.at[f, part, slot],
            send_sem=frame_send.at[f, part, peer],
            recv_sem=frame_recv.at[f, part, slot],
            device_id=(me, peer),
            device_id_type=pl.DeviceIdType.MESH,
        )

    def frame_arrival(f, part, step):
        peer = exclusive(slot, step, frame_size)
        return pltpu.make_async_remote_copy(
            src_ref=hidden.at[f, pl.ds(0, share)],
            dst_ref=gathered.at[f, part, peer],
            send_sem=frame_send.at[f, part, peer],
            recv_sem=frame_recv.at[f, part, peer],
            device_id=(me, peer),
            device_id_type=pl.DeviceIdType.MESH,
        )

    split = RELAYED * block

    def begin(f):
        for pair in range(heads):
            span = slice(pair * PAIR, (pair + 1) * PAIR)
            highest[:, span], total[:, span], count[:, span] = attend(
                query[f, :, span],
                keys[f, :split, span],
                values[f, :split, span],
                bias[:, :split],
            )

    def spatial(f, first, many):
        rows = slice(first * (block // parts), (first + many) * (block // parts))
        for pair in range(heads):
            span = slice(pair * PAIR, (pair + 1) * PAIR)
            top, more, extra = attend(
                query[f, rows, span],
                keys[f, split:, span],
                values[f, split:, span],
                bias[:, split:],
            )
            peak = jnp.maximum(highest[rows, span], top)
            old, new = jnp.exp(highest[rows, span] - peak), jnp.exp(top - peak)
            mix[rows, span] = (
                (total[rows, span] * old + more * new) / (count[rows, span] * old + extra * new)
            ).astype(BF16)
        hidden[f, rows] = (
            acts[f, rows].astype(F32)
            + jnp.dot(mix[rows], sout[...], preferred_element_type=F32)
        ).astype(BF16)
        for part in range(first, first + many):
            for step in range(frame_size - 1, 0, -1):
                frame_copy(f, part, step).start()
            mine = pl.ds(pl.multiple_of(part * (block // parts) + slot * share, 16), share)
            gathered[f, part, slot] = hidden[f, mine]

    weights[0].wait()
    for copy in weights[1:]:
        copy.start()
    for f in range(frames_dev):
        query[f] = jnp.dot(near[f, OWN], sqkv[:, :width], preferred_element_type=F32).astype(BF16)
    for f in range(frames_dev):
        for half in range(halves):
            to_mate(f, half).wait_recv()
    pass_on(0, 0)
    project(0, OWN, 2)
    pass_on(0, 1)
    project(1, OWN, 2)
    project(0, DIRECT, 1)
    begin(0)
    pass_on(1, 0)
    take_relayed(0)
    pass_on(1, 1)
    take_far(0)
    weights[1].wait()
    spatial(0, 0, parts)
    project(1, DIRECT, 1)
    begin(1)
    take_relayed(1)
    take_far(1)
    for part in range(parts):
        spatial(1, part, 1)

    def back_copy(part, peer):
        first = part * (block // parts) + slot * share
        return pltpu.make_async_remote_copy(
            src_ref=staged.at[part, peer],
            dst_ref=landed.at[:, pl.ds(pl.multiple_of(first, 16), share)],
            send_sem=back_send.at[part, peer],
            recv_sem=back_recv.at[part, slot],
            device_id=(me, peer),
            device_id_type=pl.DeviceIdType.MESH,
        )

    def back_arrival(part, peer):
        first = part * (block // parts) + peer * share
        return pltpu.make_async_remote_copy(
            src_ref=staged.at[part, peer],
            dst_ref=landed.at[:, pl.ds(pl.multiple_of(first, 16), share)],
            send_sem=back_send.at[part, peer],
            recv_sem=back_recv.at[part, peer],
            device_id=(me, peer),
            device_id_type=pl.DeviceIdType.MESH,
        )

    level = frame_size * share

    def arrive(f, part):
        for step in range(1, frame_size):
            frame_arrival(f, part, step).wait_recv()

    def time_project(f, first, many):
        renormed = normalize(gathered[f, first : first + many].reshape(many * level, width))
        span_rows = slice(f * level, (f + 1) * level)
        turning = jnp.concatenate([cosine[span_rows]] * many, axis=0)
        crossing = jnp.concatenate([sine[span_rows]] * many, axis=0)
        for third, target in ((0, tquery), (1, tkeys), (2, tvalues)):
            projected = jnp.dot(
                renormed, tqkv[:, third * width : (third + 1) * width], preferred_element_type=F32
            ).astype(BF16)
            for pair in range(heads):
                span = slice(pair * PAIR, (pair + 1) * PAIR)
                piece = projected[:, span]
                if third < 2:
                    turned = jnp.dot(piece, turn, preferred_element_type=F32)
                    piece = (piece.astype(F32) * turning + turned * crossing).astype(BF16)
                for part in range(many):
                    target[first + part, span_rows, span] = piece[part * level : (part + 1) * level]

    weights[2].wait()
    for f in range(frames_dev - 1):
        for part in range(parts):
            arrive(f, part)
        time_project(f, 0, parts)
    weights[3].wait()
    for part in range(parts):
        arrive(frames_dev - 1, part)
        time_project(frames_dev - 1, part, 1)
        for apart in range(frame_size // 2 - 1, -1, -1):
            first = 2 * exclusive(slot // 2, apart, frame_size // 2)
            rows = [
                pl.ds(pl.multiple_of(f * level + first * share, 16), 2 * share)
                for f in range(frames_dev)
            ]
            pieces = []
            for pair in range(heads):
                span = slice(pair * PAIR, (pair + 1) * PAIR)
                _, time_total, time_count = attend(
                    jnp.concatenate([tquery[part, at, span] for at in rows], axis=0),
                    tkeys[part, :, span],
                    tvalues[part, :, span],
                    same[...],
                )
                pieces.append((time_total / time_count).astype(BF16))
            time_mix = jnp.concatenate(pieces, axis=1)
            before = jnp.concatenate(
                [
                    gathered[f, part, pl.ds(first, 2)].reshape(2 * share, width)
                    for f in range(frames_dev)
                ],
                axis=0,
            )
            after = (
                before.astype(F32) + jnp.dot(time_mix, tout[...], preferred_element_type=F32)
            ).astype(BF16)
            for f in range(frames_dev):
                for d in range(2):
                    at = (2 * f + d) * share
                    staged[part, first + d, f] = after[at : at + share]
            if apart > 0:
                back_copy(part, first).start()
                back_copy(part, first + 1).start()
            else:
                back_copy(part, first + 1 - slot % 2).start()
                mine = pl.ds(pl.multiple_of(part * (block // parts) + slot * share, 16), share)
                landed[:, mine] = staged[part, slot]

    for part in range(parts):
        for step in range(1, frame_size):
            back_arrival(part, exclusive(slot, step, frame_size)).wait_recv()
    out_ref[...] = landed[...]

    for f in range(frames_dev):
        for half in range(halves):
            to_mate(f, half).wait_send()
            to_across(f, half).wait_send()

            @pl.when(gives_relay)
            def _():
                relay(f, half).wait_send()

            @pl.when(jnp.logical_or(gives_direct, gives_relayed))
            def _():
                hand_on(f, half).wait_send()

        for part in range(parts):
            for step in range(1, frame_size):
                frame_copy(f, part, step).wait_send()
    for part in range(parts):
        for step in range(1, frame_size):
            back_copy(part, exclusive(slot, step, frame_size)).wait_send()


def solution(mesh):
    res_size, frame_size = mesh.shape["res"], mesh.shape["frame"]

    def shards(activations, contacts, frame_index, spatial_qkv, spatial_out, time_qkv, time_out):
        frames_dev, block, width = activations.shape
        share = 16
        parts = block // (frame_size * share)
        frames = frames_dev * frame_size
        size = frames * share
        vmem = pl.BlockSpec(memory_space=pltpu.VMEM)
        smem = pl.BlockSpec(memory_space=pltpu.SMEM)
        hbm = pl.BlockSpec(memory_space=pltpu.HBM)
        dma = pltpu.SemaphoreType.DMA
        return pl.pallas_call(
            functools.partial(kernel, res_size, frame_size),
            out_shape=jax.ShapeDtypeStruct((frames_dev, block, width), BF16),
            in_specs=[hbm, smem, smem, hbm, hbm, hbm, hbm],
            out_specs=vmem,
            scratch_shapes=[
                pltpu.VMEM((frames_dev, block, width), BF16),
                pltpu.VMEM(spatial_qkv.shape, BF16),
                pltpu.VMEM(spatial_out.shape, BF16),
                pltpu.VMEM(time_qkv.shape, BF16),
                pltpu.VMEM(time_out.shape, BF16),
                pltpu.VMEM((frames_dev, 5, block, width), BF16),
                pltpu.VMEM((frames_dev, block, width), BF16),
                pltpu.VMEM((frames_dev, 5 * block, width), BF16),
                pltpu.VMEM((frames_dev, 5 * block, width), BF16),
                pltpu.VMEM((block, width), BF16),
                pltpu.VMEM((frames_dev, block, width), BF16),
                pltpu.VMEM((frames_dev, parts, frame_size, share, width), BF16),
                pltpu.VMEM((parts, frame_size, frames_dev, share, width), BF16),
                pltpu.VMEM((frames_dev, block, width), BF16),
                pltpu.VMEM((parts, size, width), BF16),
                pltpu.VMEM((parts, size, width), BF16),
                pltpu.VMEM((parts, size, width), BF16),
                pltpu.VMEM((size, PAIR), F32),
                pltpu.VMEM((size, PAIR), F32),
                pltpu.VMEM((4 * frames_dev * share, size), F32),
                pltpu.VMEM((block, width), F32),
                pltpu.VMEM((block, width), F32),
                pltpu.VMEM((block, width), F32),
                dma((5,)),
                dma((frames_dev, 5, 2)),
                dma((frames_dev, 5, 2)),
                dma((frames_dev, parts, frame_size)),
                dma((frames_dev, parts, frame_size)),
                dma((parts, frame_size)),
                dma((parts, frame_size)),
            ],
            compiler_params=pltpu.CompilerParams(
                collective_id=0, has_side_effects=True, vmem_limit_bytes=56 * 1024 * 1024
            ),
        )(activations, contacts, frame_index, spatial_qkv, spatial_out, time_qkv, time_out)

    placed = (P("frame", "res", None), P(), P(), P(), P(), P(), P())
    return jax.shard_map(
        shards, mesh=mesh, in_specs=placed, out_specs=P("frame", "res", None), check_vma=False
    )
```

```python
import functools
import math

import jax
import jax.numpy as jnp
from jax import lax
from jax.experimental import pallas as pl
from jax.experimental.pallas import tpu as pltpu
from jax.sharding import PartitionSpec as P

HEAD = 64
HALO = 2
PAIR = 2 * HEAD
OWN, NEAR, DIRECT, RELAYED, FAR = range(5)
F32 = jnp.float32
BF16 = jnp.bfloat16


def exclusive(first, second, size):
    bits = [1 << i for i in range(size.bit_length() - 1)]
    return sum(((first // w + second // w) % 2) * w for w in bits)


def normalize(values_in):
    widened = values_in.astype(F32)
    mean_square = jnp.mean(widened * widened, axis=-1, keepdims=True)
    return (widened * lax.rsqrt(mean_square + 1e-06)).astype(BF16)


def attend(query, keys, values, bias):
    rows = query.shape[0]
    lanes = lax.broadcasted_iota(jnp.int32, (1, PAIR), 1)
    first = jnp.where(lanes < HEAD, HEAD ** (-0.5), 0.0).astype(BF16)
    second = jnp.where(lanes < HEAD, 0.0, HEAD ** (-0.5)).astype(BF16)
    both = jnp.concatenate([query * first, query * second], axis=0)
    scores = (
        lax.dot_general(both, keys, (((1,), (1,)), ((), ())), preferred_element_type=F32) + bias
    )
    top = jnp.max(scores, axis=-1, keepdims=True)
    expo = jnp.exp(scores - top).astype(BF16)
    wide = jnp.concatenate([values, jnp.ones_like(values)], axis=1)
    mixed = jnp.dot(expo, wide, preferred_element_type=F32)
    low = lax.broadcasted_iota(jnp.int32, (rows, PAIR), 1) < HEAD
    highest = jnp.where(low, top[:rows], top[rows:])
    total = jnp.where(low, mixed[:rows, :PAIR], mixed[rows:, :PAIR])
    count = jnp.where(low, mixed[:rows, PAIR:], mixed[rows:, PAIR:])
    return highest, total, count


def kernel(
    res_size, frame_size,
    acts_in, contacts, frame_index, sqkv_in, sout_in, tqkv_in, tout_in, out_ref,
    acts, sqkv, sout, tqkv, tout, near, query, keys, values, mix, hidden, gathered, staged, landed,
    tquery, tkeys, tvalues, cosine, sine, same, highest, total, count,
    weight_sem, halo_send, halo_recv, frame_send, frame_recv, back_send, back_recv,
):
    frames_dev, block, width = acts.shape
    heads = width // PAIR
    parts, share, halves = gathered.shape[1], gathered.shape[3], halo_send.shape[2]
    frames = frames_dev * frame_size
    chunk = frames_dev * share
    me = lax.axis_index("res")
    slot = lax.axis_index("frame")
    odd = lax.rem(me, 2)
    side = lax.rem(me // 2, 2)
    mate = me + 1 - 2 * odd
    across = me + 2 - 4 * side
    relay_target = me + 4 - 8 * side
    relay_source = me - 4 + 8 * side
    gives_relay = jnp.logical_and(relay_target >= 0, relay_target < res_size)
    has_relayed = jnp.logical_and(relay_source >= 0, relay_source < res_size)
    gives_direct = side == odd
    gives_relayed = jnp.logical_and(side != odd, has_relayed)
    has_far = jnp.logical_or(side != odd, has_relayed)

    weights = [
        pltpu.make_async_copy(source, target, weight_sem.at[i])
        for i, (source, target) in enumerate(
            [(sqkv_in, sqkv), (sout_in, sout), (tqkv_in, tqkv), (tout_in, tout)]
        )
    ]
    fetch = pltpu.make_async_copy(acts_in, acts, weight_sem.at[4])
    fetch.start()
    weights[0].start()

    barrier = pltpu.get_barrier_semaphore()

    def greet(res, frame):
        pl.semaphore_signal(
            barrier, inc=1, device_id=(res, frame), device_id_type=pl.DeviceIdType.MESH
        )

    greet(mate, slot)
    greet(across, slot)

    @pl.when(gives_relay)
    def _():
        greet(relay_target, slot)

    @pl.when(has_relayed)
    def _():
        greet(relay_source, slot)

    for step in range(1, frame_size):
        greet(me, exclusive(slot, step, frame_size))

    fetch.wait()
    near[0, OWN] = normalize(acts[0])

    pl.semaphore_wait(
        barrier, frame_size + 1 + gives_relay.astype(jnp.int32) + has_relayed.astype(jnp.int32)
    )

    def halo(f, half, source, target, place):
        rows = pl.ds(half * (block // halves), block // halves)
        return pltpu.make_async_remote_copy(
            src_ref=near.at[f, source, rows],
            dst_ref=near.at[f, place, rows],
            send_sem=halo_send.at[f, place, half],
            recv_sem=halo_recv.at[f, place, half],
            device_id=(target, slot),
            device_id_type=pl.DeviceIdType.MESH,
        )

    def to_mate(f, half):
        return halo(f, half, OWN, mate, NEAR)

    def to_across(f, half):
        return halo(f, half, OWN, across, DIRECT)

    def relay(f, half):
        return halo(f, half, DIRECT, relay_target, RELAYED)

    def hand_on(f, half):
        return halo(f, half, DIRECT + side + odd - 2 * side * odd, mate, FAR)

    for f in range(frames_dev):
        if f > 0:
            near[f, OWN] = normalize(acts[f])
        for half in range(halves):
            to_across(f, half).start()
            to_mate(f, half).start()

    for place, there in ((RELAYED, has_relayed), (FAR, has_far)):

        @pl.when(jnp.logical_not(there))
        def _():
            for target in (keys, values):
                target[:, place * block : (place + 1) * block] = jnp.zeros(
                    (frames_dev, block, width), BF16
                )

    size = frames * share
    lane = lax.broadcasted_iota(jnp.int32, (frames, PAIR), 1)
    frequency = jnp.exp((lane & (HEAD // 2 - 1)).astype(F32) * (-math.log(10000.0) / (HEAD // 2)))
    position = jnp.zeros((frames, PAIR), F32)
    row = lax.broadcasted_iota(jnp.int32, (frames, PAIR), 0)
    for g in range(frames):
        at = (g % frames_dev) * frame_size + g // frames_dev
        position = jnp.where(row == at, frame_index[g].astype(F32), position)
    angle = position * frequency
    for table, entries in ((cosine, jnp.cos(angle)), (sine, jnp.sin(angle))):
        table[...] = jnp.broadcast_to(entries[:, None, :], (frames, share, PAIR)).reshape(
            size, PAIR
        )
    row = lax.broadcasted_iota(jnp.int32, same.shape, 0)
    column = lax.broadcasted_iota(jnp.int32, same.shape, 1)
    same[...] = jnp.where((row & (share - 1)) == (column & (share - 1)), 0.0, -1e30)
    row = lax.broadcasted_iota(jnp.int32, (PAIR, PAIR), 0)
    column = lax.broadcasted_iota(jnp.int32, (PAIR, PAIR), 1)
    upper = (column & (HEAD - 1)) >= HEAD // 2
    turn = jnp.where(
        upper,
        jnp.where(row == column - HEAD // 2, 1.0, 0.0),
        jnp.where(row == column + HEAD // 2, -1.0, 0.0),
    ).astype(BF16)
    order = (HALO, 3 - 2 * odd, 2 * HALO * (1 - side), 2 * HALO * side, 1 + 2 * odd)
    bias = jnp.concatenate(
        [
            jnp.full((1, block), jnp.where(contacts[me, place] > 0, 0.0, -1e30), F32)
            for place in order
        ],
        axis=1,
    )

    def project(f, first, count):
        rows = near[f, first : first + count].reshape(count * block, width)
        span = slice(first * block, (first + count) * block)
        for part, target in ((1, keys), (2, values)):
            target[f, span] = jnp.dot(
                rows, sqkv[:, part * width : (part + 1) * width], preferred_element_type=F32
            ).astype(BF16)

    def pass_on(f, half):
        to_across(f, half).wait_recv()

        @pl.when(gives_relay)
        def _():
            relay(f, half).start()

        @pl.when(gives_direct)
        def _():
            hand_on(f, half).start()

    def take_relayed(f):
        for half in range(halves):

            @pl.when(has_relayed)
            def _():
                relay(f, half).wait_recv()

            @pl.when(gives_relayed)
            def _():
                hand_on(f, half).start()

        @pl.when(has_relayed)
        def _():
            project(f, RELAYED, 1)

    def take_far(f):
        @pl.when(has_far)
        def _():
            for half in range(halves):
                hand_on(f, half).wait_recv()
            project(f, FAR, 1)

    def frame_copy(f, part, step):
        peer = exclusive(slot, step, frame_size)
        first = part * (block // parts) + peer * share
        return pltpu.make_async_remote_copy(
            src_ref=hidden.at[f, pl.ds(pl.multiple_of(first, 16), share)],
            dst_ref=gathered.at[f, part, slot],
            send_sem=frame_send.at[f, part, peer],
            recv_sem=frame_recv.at[f, part, slot],
            device_id=(me, peer),
            device_id_type=pl.DeviceIdType.MESH,
        )

    def frame_arrival(f, part, step):
        peer = exclusive(slot, step, frame_size)
        return pltpu.make_async_remote_copy(
            src_ref=hidden.at[f, pl.ds(0, share)],
            dst_ref=gathered.at[f, part, peer],
            send_sem=frame_send.at[f, part, peer],
            recv_sem=frame_recv.at[f, part, peer],
            device_id=(me, peer),
            device_id_type=pl.DeviceIdType.MESH,
        )

    split = RELAYED * block

    def begin(f):
        for pair in range(heads):
            span = slice(pair * PAIR, (pair + 1) * PAIR)
            highest[:, span], total[:, span], count[:, span] = attend(
                query[f, :, span],
                keys[f, :split, span],
                values[f, :split, span],
                bias[:, :split],
            )

    def spatial(f, first, many):
        rows = slice(first * (block // parts), (first + many) * (block // parts))
        for pair in range(heads):
            span = slice(pair * PAIR, (pair + 1) * PAIR)
            top, more, extra = attend(
                query[f, rows, span],
                keys[f, split:, span],
                values[f, split:, span],
                bias[:, split:],
            )
            peak = jnp.maximum(highest[rows, span], top)
            old, new = jnp.exp(highest[rows, span] - peak), jnp.exp(top - peak)
            mix[rows, span] = (
                (total[rows, span] * old + more * new) / (count[rows, span] * old + extra * new)
            ).astype(BF16)
        hidden[f, rows] = (
            acts[f, rows].astype(F32)
            + jnp.dot(mix[rows], sout[...], preferred_element_type=F32)
        ).astype(BF16)
        for part in range(first, first + many):
            for step in range(frame_size - 1, 0, -1):
                frame_copy(f, part, step).start()
            mine = pl.ds(pl.multiple_of(part * (block // parts) + slot * share, 16), share)
            gathered[f, part, slot] = hidden[f, mine]

    weights[0].wait()
    for copy in weights[1:]:
        copy.start()
    for f in range(frames_dev):
        query[f] = jnp.dot(near[f, OWN], sqkv[:, :width], preferred_element_type=F32).astype(BF16)
    for f in range(frames_dev):
        for half in range(halves):
            to_mate(f, half).wait_recv()
    pass_on(0, 0)
    project(0, OWN, 2)
    pass_on(0, 1)
    project(1, OWN, 2)
    project(0, DIRECT, 1)
    pass_on(1, 0)
    begin(0)
    pass_on(1, 1)
    take_relayed(0)
    take_far(0)
    weights[1].wait()
    spatial(0, 0, parts)
    project(1, DIRECT, 1)
    begin(1)
    take_relayed(1)
    take_far(1)
    for part in range(parts):
        spatial(1, part, 1)

    def back_copy(part, peer):
        first = part * (block // parts) + slot * share
        return pltpu.make_async_remote_copy(
            src_ref=staged.at[part, peer],
            dst_ref=landed.at[:, pl.ds(pl.multiple_of(first, 16), share)],
            send_sem=back_send.at[part, peer],
            recv_sem=back_recv.at[part, slot],
            device_id=(me, peer),
            device_id_type=pl.DeviceIdType.MESH,
        )

    def back_arrival(part, peer):
        first = part * (block // parts) + peer * share
        return pltpu.make_async_remote_copy(
            src_ref=staged.at[part, peer],
            dst_ref=landed.at[:, pl.ds(pl.multiple_of(first, 16), share)],
            send_sem=back_send.at[part, peer],
            recv_sem=back_recv.at[part, peer],
            device_id=(me, peer),
            device_id_type=pl.DeviceIdType.MESH,
        )

    level = frame_size * share

    def arrive(f, part):
        for step in range(1, frame_size):
            frame_arrival(f, part, step).wait_recv()

    def time_project(f, first, many):
        renormed = normalize(gathered[f, first : first + many].reshape(many * level, width))
        span_rows = slice(f * level, (f + 1) * level)
        turning = jnp.concatenate([cosine[span_rows]] * many, axis=0)
        crossing = jnp.concatenate([sine[span_rows]] * many, axis=0)
        for third, target in ((0, tquery), (1, tkeys), (2, tvalues)):
            projected = jnp.dot(
                renormed, tqkv[:, third * width : (third + 1) * width], preferred_element_type=F32
            ).astype(BF16)
            for pair in range(heads):
                span = slice(pair * PAIR, (pair + 1) * PAIR)
                piece = projected[:, span]
                if third < 2:
                    turned = jnp.dot(piece, turn, preferred_element_type=F32)
                    piece = (piece.astype(F32) * turning + turned * crossing).astype(BF16)
                for part in range(many):
                    target[first + part, span_rows, span] = piece[part * level : (part + 1) * level]

    weights[2].wait()
    for f in range(frames_dev - 1):
        for part in range(parts):
            arrive(f, part)
        time_project(f, 0, parts)
    weights[3].wait()
    for part in range(parts):
        arrive(frames_dev - 1, part)
        time_project(frames_dev - 1, part, 1)
        for apart in range(frame_size // 2 - 1, -1, -1):
            first = 2 * exclusive(slot // 2, apart, frame_size // 2)
            rows = [
                pl.ds(pl.multiple_of(f * level + first * share, 16), 2 * share)
                for f in range(frames_dev)
            ]
            pieces = []
            for pair in range(heads):
                span = slice(pair * PAIR, (pair + 1) * PAIR)
                _, time_total, time_count = attend(
                    jnp.concatenate([tquery[part, at, span] for at in rows], axis=0),
                    tkeys[part, :, span],
                    tvalues[part, :, span],
                    same[...],
                )
                pieces.append((time_total / time_count).astype(BF16))
            time_mix = jnp.concatenate(pieces, axis=1)
            before = jnp.concatenate(
                [
                    gathered[f, part, pl.ds(first, 2)].reshape(2 * share, width)
                    for f in range(frames_dev)
                ],
                axis=0,
            )
            after = (
                before.astype(F32) + jnp.dot(time_mix, tout[...], preferred_element_type=F32)
            ).astype(BF16)
            for f in range(frames_dev):
                for d in range(2):
                    at = (2 * f + d) * share
                    staged[part, first + d, f] = after[at : at + share]
            if apart > 0:
                back_copy(part, first).start()
                back_copy(part, first + 1).start()
            else:
                back_copy(part, first + 1 - slot % 2).start()
                mine = pl.ds(pl.multiple_of(part * (block // parts) + slot * share, 16), share)
                landed[:, mine] = staged[part, slot]

    for part in range(parts):
        for step in range(1, frame_size):
            back_arrival(part, exclusive(slot, step, frame_size)).wait_recv()
    out_ref[...] = landed[...]

    for f in range(frames_dev):
        for half in range(halves):
            to_mate(f, half).wait_send()
            to_across(f, half).wait_send()

            @pl.when(gives_relay)
            def _():
                relay(f, half).wait_send()

            @pl.when(jnp.logical_or(gives_direct, gives_relayed))
            def _():
                hand_on(f, half).wait_send()

        for part in range(parts):
            for step in range(1, frame_size):
                frame_copy(f, part, step).wait_send()
    for part in range(parts):
        for step in range(1, frame_size):
            back_copy(part, exclusive(slot, step, frame_size)).wait_send()


def solution(mesh):
    res_size, frame_size = mesh.shape["res"], mesh.shape["frame"]

    def shards(activations, contacts, frame_index, spatial_qkv, spatial_out, time_qkv, time_out):
        frames_dev, block, width = activations.shape
        share = 16
        parts = block // (frame_size * share)
        frames = frames_dev * frame_size
        size = frames * share
        vmem = pl.BlockSpec(memory_space=pltpu.VMEM)
        smem = pl.BlockSpec(memory_space=pltpu.SMEM)
        hbm = pl.BlockSpec(memory_space=pltpu.HBM)
        dma = pltpu.SemaphoreType.DMA
        return pl.pallas_call(
            functools.partial(kernel, res_size, frame_size),
            out_shape=jax.ShapeDtypeStruct((frames_dev, block, width), BF16),
            in_specs=[hbm, smem, smem, hbm, hbm, hbm, hbm],
            out_specs=vmem,
            scratch_shapes=[
                pltpu.VMEM((frames_dev, block, width), BF16),
                pltpu.VMEM(spatial_qkv.shape, BF16),
                pltpu.VMEM(spatial_out.shape, BF16),
                pltpu.VMEM(time_qkv.shape, BF16),
                pltpu.VMEM(time_out.shape, BF16),
                pltpu.VMEM((frames_dev, 5, block, width), BF16),
                pltpu.VMEM((frames_dev, block, width), BF16),
                pltpu.VMEM((frames_dev, 5 * block, width), BF16),
                pltpu.VMEM((frames_dev, 5 * block, width), BF16),
                pltpu.VMEM((block, width), BF16),
                pltpu.VMEM((frames_dev, block, width), BF16),
                pltpu.VMEM((frames_dev, parts, frame_size, share, width), BF16),
                pltpu.VMEM((parts, frame_size, frames_dev, share, width), BF16),
                pltpu.VMEM((frames_dev, block, width), BF16),
                pltpu.VMEM((parts, size, width), BF16),
                pltpu.VMEM((parts, size, width), BF16),
                pltpu.VMEM((parts, size, width), BF16),
                pltpu.VMEM((size, PAIR), F32),
                pltpu.VMEM((size, PAIR), F32),
                pltpu.VMEM((4 * frames_dev * share, size), F32),
                pltpu.VMEM((block, width), F32),
                pltpu.VMEM((block, width), F32),
                pltpu.VMEM((block, width), F32),
                dma((5,)),
                dma((frames_dev, 5, 2)),
                dma((frames_dev, 5, 2)),
                dma((frames_dev, parts, frame_size)),
                dma((frames_dev, parts, frame_size)),
                dma((parts, frame_size)),
                dma((parts, frame_size)),
            ],
            compiler_params=pltpu.CompilerParams(
                collective_id=0, has_side_effects=True, vmem_limit_bytes=56 * 1024 * 1024
            ),
        )(activations, contacts, frame_index, spatial_qkv, spatial_out, time_qkv, time_out)

    placed = (P("frame", "res", None), P(), P(), P(), P(), P(), P())
    return jax.shard_map(
        shards, mesh=mesh, in_specs=placed, out_specs=P("frame", "res", None), check_vma=False
    )
```

```python
import functools
import math

import jax
import jax.numpy as jnp
from jax import lax
from jax.experimental import pallas as pl
from jax.experimental.pallas import tpu as pltpu
from jax.sharding import PartitionSpec as P

HEAD = 64
HALO = 2
PAIR = 2 * HEAD
OWN, NEAR, DIRECT, RELAYED, FAR = range(5)
F32 = jnp.float32
BF16 = jnp.bfloat16


def exclusive(first, second, size):
    bits = [1 << i for i in range(size.bit_length() - 1)]
    return sum(((first // w + second // w) % 2) * w for w in bits)


def normalize(values_in):
    widened = values_in.astype(F32)
    mean_square = jnp.mean(widened * widened, axis=-1, keepdims=True)
    return (widened * lax.rsqrt(mean_square + 1e-06)).astype(BF16)


def attend(query, keys, values, bias):
    rows = query.shape[0]
    lanes = lax.broadcasted_iota(jnp.int32, (1, PAIR), 1)
    first = jnp.where(lanes < HEAD, HEAD ** (-0.5), 0.0).astype(BF16)
    second = jnp.where(lanes < HEAD, 0.0, HEAD ** (-0.5)).astype(BF16)
    both = jnp.concatenate([query * first, query * second], axis=0)
    scores = (
        lax.dot_general(both, keys, (((1,), (1,)), ((), ())), preferred_element_type=F32) + bias
    )
    top = jnp.max(scores, axis=-1, keepdims=True)
    expo = jnp.exp(scores - top).astype(BF16)
    wide = jnp.concatenate([values, jnp.ones_like(values)], axis=1)
    mixed = jnp.dot(expo, wide, preferred_element_type=F32)
    low = lax.broadcasted_iota(jnp.int32, (rows, PAIR), 1) < HEAD
    highest = jnp.where(low, top[:rows], top[rows:])
    total = jnp.where(low, mixed[:rows, :PAIR], mixed[rows:, :PAIR])
    count = jnp.where(low, mixed[:rows, PAIR:], mixed[rows:, PAIR:])
    return highest, total, count


def kernel(
    res_size, frame_size,
    acts_in, contacts, frame_index, sqkv_in, sout_in, tqkv_in, tout_in, out_ref,
    acts, sqkv, sout, tqkv, tout, near, query, keys, values, mix, hidden, gathered, staged, landed,
    tquery, tkeys, tvalues, cosine, sine, same, highest, total, count,
    weight_sem, halo_send, halo_recv, frame_send, frame_recv, back_send, back_recv,
):
    frames_dev, block, width = acts.shape
    heads = width // PAIR
    parts, share, halves = gathered.shape[1], gathered.shape[3], halo_send.shape[2]
    frames = frames_dev * frame_size
    chunk = frames_dev * share
    me = lax.axis_index("res")
    slot = lax.axis_index("frame")
    odd = lax.rem(me, 2)
    side = lax.rem(me // 2, 2)
    mate = me + 1 - 2 * odd
    across = me + 2 - 4 * side
    relay_target = me + 4 - 8 * side
    relay_source = me - 4 + 8 * side
    gives_relay = jnp.logical_and(relay_target >= 0, relay_target < res_size)
    has_relayed = jnp.logical_and(relay_source >= 0, relay_source < res_size)
    gives_direct = side == odd
    gives_relayed = jnp.logical_and(side != odd, has_relayed)
    has_far = jnp.logical_or(side != odd, has_relayed)

    weights = [
        pltpu.make_async_copy(source, target, weight_sem.at[i])
        for i, (source, target) in enumerate(
            [(sqkv_in, sqkv), (sout_in, sout), (tqkv_in, tqkv), (tout_in, tout)]
        )
    ]
    fetch = pltpu.make_async_copy(acts_in, acts, weight_sem.at[4])
    fetch.start()
    weights[0].start()

    barrier = pltpu.get_barrier_semaphore()

    def greet(res, frame):
        pl.semaphore_signal(
            barrier, inc=1, device_id=(res, frame), device_id_type=pl.DeviceIdType.MESH
        )

    greet(mate, slot)
    greet(across, slot)

    @pl.when(gives_relay)
    def _():
        greet(relay_target, slot)

    @pl.when(has_relayed)
    def _():
        greet(relay_source, slot)

    for step in range(1, frame_size):
        greet(me, exclusive(slot, step, frame_size))

    fetch.wait()
    near[0, OWN] = normalize(acts[0])

    pl.semaphore_wait(
        barrier, frame_size + 1 + gives_relay.astype(jnp.int32) + has_relayed.astype(jnp.int32)
    )

    def halo(f, half, source, target, place):
        rows = pl.ds(half * (block // halves), block // halves)
        return pltpu.make_async_remote_copy(
            src_ref=near.at[f, source, rows],
            dst_ref=near.at[f, place, rows],
            send_sem=halo_send.at[f, place, half],
            recv_sem=halo_recv.at[f, place, half],
            device_id=(target, slot),
            device_id_type=pl.DeviceIdType.MESH,
        )

    def to_mate(f, half):
        return halo(f, half, OWN, mate, NEAR)

    def to_across(f, half):
        return halo(f, half, OWN, across, DIRECT)

    def relay(f, half):
        return halo(f, half, DIRECT, relay_target, RELAYED)

    def hand_on(f, half):
        return halo(f, half, DIRECT + side + odd - 2 * side * odd, mate, FAR)

    for f in range(frames_dev):
        if f > 0:
            near[f, OWN] = normalize(acts[f])
        for half in range(halves):
            to_across(f, half).start()
            to_mate(f, half).start()

    for place, there in ((RELAYED, has_relayed), (FAR, has_far)):

        @pl.when(jnp.logical_not(there))
        def _():
            for target in (keys, values):
                target[:, place * block : (place + 1) * block] = jnp.zeros(
                    (frames_dev, block, width), BF16
                )

    size = frames * share
    lane = lax.broadcasted_iota(jnp.int32, (frames, PAIR), 1)
    frequency = jnp.exp((lane & (HEAD // 2 - 1)).astype(F32) * (-math.log(10000.0) / (HEAD // 2)))
    position = jnp.zeros((frames, PAIR), F32)
    row = lax.broadcasted_iota(jnp.int32, (frames, PAIR), 0)
    for g in range(frames):
        at = (g % frames_dev) * frame_size + g // frames_dev
        position = jnp.where(row == at, frame_index[g].astype(F32), position)
    angle = position * frequency
    for table, entries in ((cosine, jnp.cos(angle)), (sine, jnp.sin(angle))):
        table[...] = jnp.broadcast_to(entries[:, None, :], (frames, share, PAIR)).reshape(
            size, PAIR
        )
    row = lax.broadcasted_iota(jnp.int32, same.shape, 0)
    column = lax.broadcasted_iota(jnp.int32, same.shape, 1)
    same[...] = jnp.where((row & (share - 1)) == (column & (share - 1)), 0.0, -1e30)
    row = lax.broadcasted_iota(jnp.int32, (PAIR, PAIR), 0)
    column = lax.broadcasted_iota(jnp.int32, (PAIR, PAIR), 1)
    upper = (column & (HEAD - 1)) >= HEAD // 2
    turn = jnp.where(
        upper,
        jnp.where(row == column - HEAD // 2, 1.0, 0.0),
        jnp.where(row == column + HEAD // 2, -1.0, 0.0),
    ).astype(BF16)
    order = (HALO, 3 - 2 * odd, 2 * HALO * (1 - side), 2 * HALO * side, 1 + 2 * odd)
    bias = jnp.concatenate(
        [
            jnp.full((1, block), jnp.where(contacts[me, place] > 0, 0.0, -1e30), F32)
            for place in order
        ],
        axis=1,
    )

    def project(f, first, count):
        rows = near[f, first : first + count].reshape(count * block, width)
        span = slice(first * block, (first + count) * block)
        for part, target in ((1, keys), (2, values)):
            target[f, span] = jnp.dot(
                rows, sqkv[:, part * width : (part + 1) * width], preferred_element_type=F32
            ).astype(BF16)

    def pass_on(f, half):
        to_across(f, half).wait_recv()

        @pl.when(gives_relay)
        def _():
            relay(f, half).start()

        @pl.when(gives_direct)
        def _():
            hand_on(f, half).start()

    def take_relayed(f):
        for half in range(halves):

            @pl.when(has_relayed)
            def _():
                relay(f, half).wait_recv()

            @pl.when(gives_relayed)
            def _():
                hand_on(f, half).start()

        @pl.when(has_relayed)
        def _():
            project(f, RELAYED, 1)

    def take_far(f):
        @pl.when(has_far)
        def _():
            for half in range(halves):
                hand_on(f, half).wait_recv()
            project(f, FAR, 1)

    def frame_copy(f, part, step):
        peer = exclusive(slot, step, frame_size)
        first = part * (block // parts) + peer * share
        return pltpu.make_async_remote_copy(
            src_ref=hidden.at[f, pl.ds(pl.multiple_of(first, 16), share)],
            dst_ref=gathered.at[f, part, slot],
            send_sem=frame_send.at[f, part, peer],
            recv_sem=frame_recv.at[f, part, slot],
            device_id=(me, peer),
            device_id_type=pl.DeviceIdType.MESH,
        )

    def frame_arrival(f, part, step):
        peer = exclusive(slot, step, frame_size)
        return pltpu.make_async_remote_copy(
            src_ref=hidden.at[f, pl.ds(0, share)],
            dst_ref=gathered.at[f, part, peer],
            send_sem=frame_send.at[f, part, peer],
            recv_sem=frame_recv.at[f, part, peer],
            device_id=(me, peer),
            device_id_type=pl.DeviceIdType.MESH,
        )

    split = RELAYED * block

    def begin(f):
        for pair in range(heads):
            span = slice(pair * PAIR, (pair + 1) * PAIR)
            highest[:, span], total[:, span], count[:, span] = attend(
                query[f, :, span],
                keys[f, :split, span],
                values[f, :split, span],
                bias[:, :split],
            )

    def spatial(f, first, many):
        rows = slice(first * (block // parts), (first + many) * (block // parts))
        for pair in range(heads):
            span = slice(pair * PAIR, (pair + 1) * PAIR)
            top, more, extra = attend(
                query[f, rows, span],
                keys[f, split:, span],
                values[f, split:, span],
                bias[:, split:],
            )
            peak = jnp.maximum(highest[rows, span], top)
            old, new = jnp.exp(highest[rows, span] - peak), jnp.exp(top - peak)
            mix[rows, span] = (
                (total[rows, span] * old + more * new) / (count[rows, span] * old + extra * new)
            ).astype(BF16)
        hidden[f, rows] = (
            acts[f, rows].astype(F32)
            + jnp.dot(mix[rows], sout[...], preferred_element_type=F32)
        ).astype(BF16)
        for part in range(first, first + many):
            for step in range(frame_size - 1, 0, -1):
                frame_copy(f, part, step).start()
            mine = pl.ds(pl.multiple_of(part * (block // parts) + slot * share, 16), share)
            gathered[f, part, slot] = hidden[f, mine]

    weights[0].wait()
    for copy in weights[1:]:
        copy.start()
    for f in range(frames_dev):
        query[f] = jnp.dot(near[f, OWN], sqkv[:, :width], preferred_element_type=F32).astype(BF16)
    for f in range(frames_dev):
        for half in range(halves):
            to_mate(f, half).wait_recv()
    pass_on(0, 0)
    project(0, OWN, 2)
    pass_on(0, 1)
    project(1, OWN, 2)
    project(0, DIRECT, 1)
    pass_on(1, 0)
    begin(0)
    pass_on(1, 1)
    project(1, DIRECT, 1)
    take_relayed(0)
    take_far(0)
    weights[1].wait()
    spatial(0, 0, parts)
    begin(1)
    take_relayed(1)
    take_far(1)
    for part in range(parts):
        spatial(1, part, 1)

    def back_copy(part, peer):
        first = part * (block // parts) + slot * share
        return pltpu.make_async_remote_copy(
            src_ref=staged.at[part, peer],
            dst_ref=landed.at[:, pl.ds(pl.multiple_of(first, 16), share)],
            send_sem=back_send.at[part, peer],
            recv_sem=back_recv.at[part, slot],
            device_id=(me, peer),
            device_id_type=pl.DeviceIdType.MESH,
        )

    def back_arrival(part, peer):
        first = part * (block // parts) + peer * share
        return pltpu.make_async_remote_copy(
            src_ref=staged.at[part, peer],
            dst_ref=landed.at[:, pl.ds(pl.multiple_of(first, 16), share)],
            send_sem=back_send.at[part, peer],
            recv_sem=back_recv.at[part, peer],
            device_id=(me, peer),
            device_id_type=pl.DeviceIdType.MESH,
        )

    level = frame_size * share

    def arrive(f, part):
        for step in range(1, frame_size):
            frame_arrival(f, part, step).wait_recv()

    def time_project(f, first, many):
        renormed = normalize(gathered[f, first : first + many].reshape(many * level, width))
        span_rows = slice(f * level, (f + 1) * level)
        turning = jnp.concatenate([cosine[span_rows]] * many, axis=0)
        crossing = jnp.concatenate([sine[span_rows]] * many, axis=0)
        for third, target in ((0, tquery), (1, tkeys), (2, tvalues)):
            projected = jnp.dot(
                renormed, tqkv[:, third * width : (third + 1) * width], preferred_element_type=F32
            ).astype(BF16)
            for pair in range(heads):
                span = slice(pair * PAIR, (pair + 1) * PAIR)
                piece = projected[:, span]
                if third < 2:
                    turned = jnp.dot(piece, turn, preferred_element_type=F32)
                    piece = (piece.astype(F32) * turning + turned * crossing).astype(BF16)
                for part in range(many):
                    target[first + part, span_rows, span] = piece[part * level : (part + 1) * level]

    weights[2].wait()
    for f in range(frames_dev - 1):
        for part in range(parts):
            arrive(f, part)
        time_project(f, 0, parts)
    weights[3].wait()
    for part in range(parts):
        arrive(frames_dev - 1, part)
        time_project(frames_dev - 1, part, 1)
        for apart in range(frame_size // 2 - 1, -1, -1):
            first = 2 * exclusive(slot // 2, apart, frame_size // 2)
            rows = [
                pl.ds(pl.multiple_of(f * level + first * share, 16), 2 * share)
                for f in range(frames_dev)
            ]
            pieces = []
            for pair in range(heads):
                span = slice(pair * PAIR, (pair + 1) * PAIR)
                _, time_total, time_count = attend(
                    jnp.concatenate([tquery[part, at, span] for at in rows], axis=0),
                    tkeys[part, :, span],
                    tvalues[part, :, span],
                    same[...],
                )
                pieces.append((time_total / time_count).astype(BF16))
            time_mix = jnp.concatenate(pieces, axis=1)
            before = jnp.concatenate(
                [
                    gathered[f, part, pl.ds(first, 2)].reshape(2 * share, width)
                    for f in range(frames_dev)
                ],
                axis=0,
            )
            after = (
                before.astype(F32) + jnp.dot(time_mix, tout[...], preferred_element_type=F32)
            ).astype(BF16)
            for f in range(frames_dev):
                for d in range(2):
                    at = (2 * f + d) * share
                    staged[part, first + d, f] = after[at : at + share]
            if apart > 0:
                back_copy(part, first).start()
                back_copy(part, first + 1).start()
            else:
                back_copy(part, first + 1 - slot % 2).start()
                mine = pl.ds(pl.multiple_of(part * (block // parts) + slot * share, 16), share)
                landed[:, mine] = staged[part, slot]

    for part in range(parts):
        for step in range(1, frame_size):
            back_arrival(part, exclusive(slot, step, frame_size)).wait_recv()
    out_ref[...] = landed[...]

    for f in range(frames_dev):
        for half in range(halves):
            to_mate(f, half).wait_send()
            to_across(f, half).wait_send()

            @pl.when(gives_relay)
            def _():
                relay(f, half).wait_send()

            @pl.when(jnp.logical_or(gives_direct, gives_relayed))
            def _():
                hand_on(f, half).wait_send()

        for part in range(parts):
            for step in range(1, frame_size):
                frame_copy(f, part, step).wait_send()
    for part in range(parts):
        for step in range(1, frame_size):
            back_copy(part, exclusive(slot, step, frame_size)).wait_send()


def solution(mesh):
    res_size, frame_size = mesh.shape["res"], mesh.shape["frame"]

    def shards(activations, contacts, frame_index, spatial_qkv, spatial_out, time_qkv, time_out):
        frames_dev, block, width = activations.shape
        share = 16
        parts = block // (frame_size * share)
        frames = frames_dev * frame_size
        size = frames * share
        vmem = pl.BlockSpec(memory_space=pltpu.VMEM)
        smem = pl.BlockSpec(memory_space=pltpu.SMEM)
        hbm = pl.BlockSpec(memory_space=pltpu.HBM)
        dma = pltpu.SemaphoreType.DMA
        return pl.pallas_call(
            functools.partial(kernel, res_size, frame_size),
            out_shape=jax.ShapeDtypeStruct((frames_dev, block, width), BF16),
            in_specs=[hbm, smem, smem, hbm, hbm, hbm, hbm],
            out_specs=vmem,
            scratch_shapes=[
                pltpu.VMEM((frames_dev, block, width), BF16),
                pltpu.VMEM(spatial_qkv.shape, BF16),
                pltpu.VMEM(spatial_out.shape, BF16),
                pltpu.VMEM(time_qkv.shape, BF16),
                pltpu.VMEM(time_out.shape, BF16),
                pltpu.VMEM((frames_dev, 5, block, width), BF16),
                pltpu.VMEM((frames_dev, block, width), BF16),
                pltpu.VMEM((frames_dev, 5 * block, width), BF16),
                pltpu.VMEM((frames_dev, 5 * block, width), BF16),
                pltpu.VMEM((block, width), BF16),
                pltpu.VMEM((frames_dev, block, width), BF16),
                pltpu.VMEM((frames_dev, parts, frame_size, share, width), BF16),
                pltpu.VMEM((parts, frame_size, frames_dev, share, width), BF16),
                pltpu.VMEM((frames_dev, block, width), BF16),
                pltpu.VMEM((parts, size, width), BF16),
                pltpu.VMEM((parts, size, width), BF16),
                pltpu.VMEM((parts, size, width), BF16),
                pltpu.VMEM((size, PAIR), F32),
                pltpu.VMEM((size, PAIR), F32),
                pltpu.VMEM((4 * frames_dev * share, size), F32),
                pltpu.VMEM((block, width), F32),
                pltpu.VMEM((block, width), F32),
                pltpu.VMEM((block, width), F32),
                dma((5,)),
                dma((frames_dev, 5, 2)),
                dma((frames_dev, 5, 2)),
                dma((frames_dev, parts, frame_size)),
                dma((frames_dev, parts, frame_size)),
                dma((parts, frame_size)),
                dma((parts, frame_size)),
            ],
            compiler_params=pltpu.CompilerParams(
                collective_id=0, has_side_effects=True, vmem_limit_bytes=56 * 1024 * 1024
            ),
        )(activations, contacts, frame_index, spatial_qkv, spatial_out, time_qkv, time_out)

    placed = (P("frame", "res", None), P(), P(), P(), P(), P(), P())
    return jax.shard_map(
        shards, mesh=mesh, in_specs=placed, out_specs=P("frame", "res", None), check_vma=False
    )
```
